128 devices in a mesh: region: 128 (over y, z, x, core).
Axes of the slice: x: 4, y: 4, z: 4, core: 2. Of those that a mesh axis runs over, the one named last changes fastest.
Arguments:
- fields: bfloat16 [6144, 12, 32, 128], P('region'), may hold values from -6 to 6
- weights: bfloat16 [6144, 8, 128, 128], P('region'), may hold values from -0.1875 to 0.1875
- departures: int32 [6144, 8], P('region'), may hold values from 0 to 6143, as said below
Outputs:
- advected: bfloat16 [6144, 12, 32, 128], P('region')
The draws below stay inside these ranges and needn't reach their ends.
Inputs may be any that keep to these rules, and one draw needn't show every extreme that they name: `departures`: blocks of device d are 48 * d to 48 * d + 47. Among the 384 slots of one device, the blocks of each other device are named by either no slot or exactly 2 slots; the two devices next to it (indices modulo 128) are always named, and on some device every other device is named.
All inputs are finite; a program needn't handle non-finite values.
Results may differ from the reference program's by a relative error of at most 0.001.
Values may be sent and summed in bfloat16 or wider, within the bound.
A program may use at most 192 MiB of HBM per device.

```python
import jax
import jax.numpy as jnp
from jax import lax

FIELDS = 12
LEV = 32
COLS = 128
S = 8
CAP = 2
BLK_DEV = 48
NBLK = 6144
N_REGION = 128


def draw_departures(key, part):
    key = jax.random.fold_in(key, 11)
    peer_count = N_REGION
    slot_total = BLK_DEV * S
    key_centre, key_perm, key_local = jax.random.split(key, 3)
    centre = jax.random.randint(key_centre, (), 0, peer_count)
    device_ids = jnp.arange(peer_count, dtype=jnp.int32)
    raw_gap = jnp.abs(device_ids - centre)
    cycle_dist = jnp.minimum(raw_gap, peer_count - raw_gap)
    half_cycle = peer_count // 2
    base_peers = peer_count // 4
    top_peers = peer_count - 1
    peer_total = base_peers + (top_peers - base_peers) * (half_cycle - cycle_dist) ** 2 // (half_cycle * half_cycle)

    def one_device(sub_key):
        key_far, key_order = jax.random.split(sub_key)
        far_offsets = jax.random.permutation(key_far, peer_count - 3).astype(jnp.int32) + 2
        offsets = jnp.concatenate([jnp.array([1, peer_count - 1], jnp.int32), far_offsets])
        slot_order = jax.random.permutation(key_order, slot_total).astype(jnp.int32)
        return (offsets, slot_order)
    offsets, slot_order = jax.vmap(one_device)(jax.random.split(key_perm, peer_count))
    position = jnp.arange(slot_total, dtype=jnp.int32)
    group_ids = position // CAP
    group_clip = jnp.minimum(group_ids, peer_count - 2)
    offset_at = jnp.take_along_axis(offsets, jnp.broadcast_to(group_clip[None, :], (peer_count, slot_total)), axis=1)
    offset_at = jnp.where(group_ids[None, :] < peer_total[:, None], offset_at, 0)
    offset_slot = jnp.take_along_axis(offset_at, slot_order, axis=1)
    owner_dev = (device_ids[:, None] + offset_slot) % peer_count
    local_idx = jax.random.randint(key_local, (peer_count, slot_total), 0, BLK_DEV)
    block_ids = owner_dev * BLK_DEV + local_idx
    return block_ids.reshape(peer_count * BLK_DEV, S).astype(jnp.int32)


def block_scale(rng, shape, cuts, low, high):
    loudness = 1.0
    for dim, blocks in cuts:
        draws = jax.random.uniform(jax.random.fold_in(jax.random.fold_in(rng, 6), dim), (blocks,), jnp.float32, low / len(cuts), high / len(cuts))
        loudness = loudness * jnp.repeat(jnp.exp(draws), shape[dim] // blocks).reshape((-1,) + (1,) * (len(shape) - 1 - dim))
    return loudness


def normal_values(stream_key, dims, scale, bound, cuts=(), kind=jnp.bfloat16):
    values = jax.random.normal(stream_key, dims, jnp.float32) * scale
    if len(cuts) > 0:
        values = block_scale(stream_key, dims, cuts, -0.22, 0.18) * values
    return jnp.clip(values, min=-bound, max=bound).astype(kind)


def setup_inputs(seed: int = 0) -> dict:
    splits = jax.random.split(jax.random.key(seed), 4)
    fields = normal_values(splits[0], (NBLK, FIELDS, LEV, COLS), 1.0, 6.0, ((0, 128),))
    weights = normal_values(splits[1], (NBLK, S, COLS, COLS), (S * COLS) ** -0.5, 0.1875, ((0, 128),))
    departures = draw_departures(jax.random.fold_in(splits[3], 71), 0)
    return dict(fields=fields, weights=weights, departures=departures)


def reference(fields, weights, departures):
    groups = departures.shape[0] // BLK_DEV

    def one_group(items):
        pick_ids, tile_group = items
        picked = fields[pick_ids].astype(jnp.float32)
        result = jnp.einsum("bsflk,bskc->bflc", picked, tile_group.astype(jnp.float32))
        return result.astype(jnp.bfloat16)

    result = lax.map(one_group, (departures.reshape(groups, BLK_DEV, S), weights.reshape(groups, BLK_DEV, S, COLS, COLS)))
    return result.reshape(fields.shape)
```

```python
import functools

import jax
import jax.numpy as jnp
from jax import lax
from jax.experimental import pallas as pl
from jax.experimental.pallas import tpu as pltpu
from jax.sharding import PartitionSpec as P

MESH = pl.DeviceIdType.MESH
SIDE = 4
PEERS = 128
GROUPS = 3
PHASES = 2
PICKS = 2
REMOTE = PEERS * PICKS


def coords(device):
    return [device // 32, (device // 8) % 4, (device // 2) % 4, device % 2]


def index_of(position):
    y, z, x, core = position
    return ((y * 4 + z) * 4 + x) * 2 + core


def shifted(position, axis, steps, core_flip=0):
    moved = list(position)
    moved[axis] = (moved[axis] + steps) % SIDE
    if core_flip:
        moved[3] = 1 - moved[3]
    return index_of(moved)


def exchange_kernel(wants, fields, pool, landing, *scratch):
    count = GROUPS * PHASES
    near = [scratch[i * SIDE : (i + 1) * SIDE] for i in range(count)]
    bundle = scratch[count * SIDE : count * SIDE + count]
    own_sem, a_send, a_recv, b_send, b_recv, c_send, c_recv, keep_sem = scratch[count * SIDE + count :]
    blocks = fields.shape[0]
    half = blocks // 2
    rows = fields.shape[2] // PHASES
    me = lax.axis_index("region")
    here = coords(me)

    peers = [shifted(here, axis, steps, flip) for axis in range(3) for steps in (1, 2, 3) for flip in (0, 1)]
    peers.append(shifted(here, 0, 0, 1))
    barrier = pltpu.get_barrier_semaphore()
    for peer in peers:
        pl.semaphore_signal(barrier, inc=1, device_id=(peer,), device_id_type=MESH)
    pl.semaphore_wait(barrier, len(peers))

    def send(src, dst, send_sem, recv_sem, device):
        copy = pltpu.make_async_remote_copy(
            src_ref=src, dst_ref=dst, send_sem=send_sem, recv_sem=recv_sem, device_id=(device,), device_id_type=MESH
        )
        copy.start()
        return copy

    low, high = pl.ds(0, half), pl.ds(half, half)

    def start_gather(k):
        phase, group = divmod(k, GROUPS)
        part = pl.ds(phase * rows, rows)
        up, down = shifted(here, group, 1), shifted(here, group, 3)
        own = pltpu.make_async_copy(fields.at[:, group, part, :], near[k][0], own_sem.at[k])
        own.start()
        plan = (
            (low, near[k][3], up),
            (high, near[k][1], down),
            (high, near[k][3], up),
            (low, near[k][1], down),
        )
        copies = [
            send(fields.at[span, group, part, :], dst.at[span], a_send.at[k, i], a_recv.at[k, i], device)
            for i, (span, dst, device) in enumerate(plan)
        ]
        return own, copies

    def relay_gather(k, copies):
        group = k % GROUPS
        up, down = shifted(here, group, 1), shifted(here, group, 3)
        copies[0].wait_recv()
        copies.append(send(near[k][3].at[low], near[k][2].at[low], a_send.at[k, 4], a_recv.at[k, 4], up))
        copies[1].wait_recv()
        copies.append(send(near[k][1].at[high], near[k][2].at[high], a_send.at[k, 5], a_recv.at[k, 5], down))

    def pick(k, ja, tb):
        group = k % GROUPS
        axis_a, axis_b, axis_c = group, (group + 1) % 3, (group + 2) % 3
        source = list(here)
        source[axis_a] = (source[axis_a] + ja) % SIDE
        column = index_of(source) * PICKS

        def one(t, carry):
            target = list(here)
            target[axis_b] = (target[axis_b] + tb) % SIDE
            target[axis_c] = (target[axis_c] + t // 2) % SIDE
            target[3] = (target[3] + t) % 2
            row = index_of(target)
            for r in range(PICKS):
                bundle[k][tb, t, ja, r] = near[k][ja][wants[row, column + r]]
            return carry

        lax.fori_loop(0, 2 * SIDE, one, 0)

    def finish_gather(k, own, copies):
        own.wait()
        for tb in range(SIDE):
            pick(k, 0, tb)
        copies[3].wait_recv()
        for tb in range(SIDE):
            pick(k, 1, tb)
        copies[2].wait_recv()
        for tb in range(SIDE):
            pick(k, 3, tb)
        copies[4].wait_recv()
        copies[5].wait_recv()

    def last_pick_and_send(k):
        phase, group = divmod(k, GROUPS)
        axis_b = (group + 1) % 3
        copies = {}
        for tb in (2, 1, 3, 0):
            pick(k, 2, tb)
            if tb:
                jb = SIDE - tb
                copies[jb] = send(
                    bundle[k].at[tb],
                    landing.at[phase, group, jb - 1],
                    b_send.at[k, tb - 1],
                    b_recv.at[k, jb - 1],
                    shifted(here, axis_b, tb),
                )
        return copies

    def home(k, jb, jc, jcore):
        phase, group = divmod(k, GROUPS)
        place = [None] * 3
        place[group] = slice(None)
        place[(group + 1) % 3] = jb
        place[(group + 2) % 3] = jc
        return pool.at[(phase, group) + tuple(place) + (jcore,)]

    def send_on(k, jb):
        phase, group = divmod(k, GROUPS)
        axis_c = (group + 2) % 3
        for t in (4, 5, 2, 3, 6, 7, 1, 0):
            tc, flip = divmod(t, 2)
            src = bundle[k].at[0, t] if jb == 0 else landing.at[phase, group, jb - 1, t]
            dst = home(k, jb, (SIDE - tc) % SIDE, flip)
            if t == 0:
                pltpu.make_async_copy(src, dst, keep_sem.at[k, jb]).start()
            else:
                send(src, dst, c_send.at[k, t - 1], c_recv.at[k, (SIDE - tc) % SIDE], shifted(here, axis_c, tc, flip))

    def column(k, jc, cores):
        phase, group = divmod(k, GROUPS)
        place = [slice(None)] * 3
        place[(group + 2) % 3] = jc
        return pool.at[(phase, group) + tuple(place) + (cores,)]

    def drain(k):
        for jc in range(SIDE):
            ref = column(k, jc, slice(None) if jc else 1)
            pltpu.make_async_copy(ref, ref, c_recv.at[k, jc]).wait()
        for t in range(1, 2 * SIDE):
            ref = column(k, 0, 0)
            pltpu.make_async_copy(ref, ref, c_send.at[k, t - 1]).wait()
        for jb in range(SIDE):
            ref = home(k, jb, 0, 0)
            pltpu.make_async_copy(ref, ref, keep_sem.at[k, jb]).wait()

    gathered, along = {}, {}
    first = range(GROUPS)
    for k in first:
        gathered[k] = start_gather(k)
    for phase in range(PHASES):
        ks = range(phase * GROUPS, (phase + 1) * GROUPS)
        for k in ks:
            relay_gather(k, gathered[k][1])
        for k in ks:
            finish_gather(k, *gathered[k])
            if phase + 1 < PHASES:
                gathered[k + GROUPS] = start_gather(k + GROUPS)
        for k in ks:
            along[k] = last_pick_and_send(k)
            send_on(k, 0)
    for k in range(count):
        for jb in (1, 3, 2):
            along[k][jb].wait_recv()
            send_on(k, jb)
    for k in range(count):
        drain(k)
        for copy in gathered[k][1]:
            copy.wait_send()
        for copy in along[k].values():
            copy.wait_send()


def exchange(wants, fields):
    blocks, _, group_rows, cols = fields.shape
    rows = group_rows // PHASES
    count = GROUPS * PHASES
    kind = fields.dtype
    dma = pltpu.SemaphoreType.DMA
    any_spec = pl.BlockSpec(memory_space=pl.ANY)
    scratch = [pltpu.VMEM((blocks, rows, cols), kind) for _ in range(count * SIDE)]
    scratch += [pltpu.VMEM((SIDE, 2 * SIDE, SIDE, PICKS, rows, cols), kind) for _ in range(count)]
    scratch += [
        dma((count,)),
        dma((count, 6)),
        dma((count, 6)),
        dma((count, 3)),
        dma((count, 3)),
        dma((count, 7)),
        dma((count, SIDE)),
        dma((count, SIDE)),
    ]
    pool, _ = pl.pallas_call(
        exchange_kernel,
        out_shape=(
            jax.ShapeDtypeStruct((PHASES, GROUPS, SIDE, SIDE, SIDE, 2, PICKS, rows, cols), kind),
            jax.ShapeDtypeStruct((PHASES, GROUPS, SIDE - 1, 2 * SIDE, SIDE, PICKS, rows, cols), kind),
        ),
        in_specs=[pl.BlockSpec(memory_space=pltpu.SMEM), any_spec],
        out_specs=(any_spec, any_spec),
        scratch_shapes=scratch,
        compiler_params=pltpu.CompilerParams(
            collective_id=0, has_side_effects=True, vmem_limit_bytes=56 * 1024 * 1024
        ),
    )(wants, fields)
    return pool.reshape(PHASES, GROUPS, REMOTE, rows, cols)


def interpolate_kernel(picks, pool, fields, weights, out):
    slots = weights.shape[1]
    cols = weights.shape[2]

    def one(b, carry):
        total = None
        for s in range(0, slots, 2):
            pair = []
            for i in (s, s + 1):
                pick = picks[b, i]
                away = pool[0, 0, jnp.minimum(pick, REMOTE - 1)]
                local = fields[jnp.maximum(pick - REMOTE, 0), 0, 0]
                pair.append(jnp.where(pick < REMOTE, away, local))
            left = jnp.concatenate(pair, axis=1)
            right = weights[b, s : s + 2].reshape(2 * cols, cols)
            part = jnp.dot(left, right, preferred_element_type=jnp.float32)
            total = part if total is None else total + part
        out[b, 0, 0] = total.astype(out.dtype)
        return carry

    lax.fori_loop(0, weights.shape[0], one, 0)


def interpolate(picks, pool, fields, weights):
    blocks, _, group_rows, cols = fields.shape
    rows = group_rows // PHASES
    split = fields.reshape(blocks, GROUPS, PHASES, rows, cols)
    part = pl.BlockSpec((blocks, 1, 1, rows, cols), lambda p, g: (0, g, p, 0, 0))
    return pl.pallas_call(
        interpolate_kernel,
        grid=(PHASES, GROUPS),
        out_shape=jax.ShapeDtypeStruct(split.shape, fields.dtype),
        in_specs=[
            pl.BlockSpec(memory_space=pltpu.SMEM),
            pl.BlockSpec((1, 1, REMOTE, rows, cols), lambda p, g: (p, g, 0, 0, 0)),
            part,
            pl.BlockSpec(weights.shape, lambda p, g: (0, 0, 0, 0), pipeline_mode=pl.Buffered(1)),
        ],
        out_specs=part,
        compiler_params=pltpu.CompilerParams(vmem_limit_bytes=56 * 1024 * 1024),
    )(picks, pool, split, weights)


def tables(departures, blocks):
    me = lax.axis_index("region")
    flat = departures.reshape(-1)
    owner = flat // blocks
    local = flat % blocks
    key = jnp.arange(flat.shape[0], dtype=jnp.int32) * 64 + local
    named = owner[None, :] == jnp.arange(PEERS, dtype=jnp.int32)[:, None]
    first = jnp.min(jnp.where(named, key[None, :], 1 << 30), axis=1)
    last = jnp.max(jnp.where(named, key[None, :], 0), axis=1)
    wants = jnp.stack([jnp.where(first < (1 << 30), first, 0) % 64, last % 64], axis=1)
    is_first = jnp.any(named & (key[None, :] == first[:, None]), axis=0)
    rank = jnp.where(is_first, 0, 1)
    there, here = coords(owner), coords(me)
    offset = [(there[i] - here[i]) % SIDE for i in range(3)] + [(there[3] - here[3]) % 2]
    picks = jnp.where(owner == me, REMOTE + local, index_of(offset) * PICKS + rank)
    return wants, picks.reshape(departures.shape)


def on_device(fields, weights, departures):
    blocks, field_count, levels, cols = fields.shape
    grouped = fields.reshape(blocks, GROUPS, field_count // GROUPS * levels, cols)
    wants, picks = tables(departures, blocks)
    wants = lax.all_gather(wants.reshape(-1), "region", axis=0)
    pool = exchange(wants, grouped)
    return interpolate(picks, pool, grouped, weights).reshape(fields.shape)


def solution(mesh):
    in_specs = (P("region", None, None, None), P("region", None, None, None), P("region", None))
    out_specs = P("region", None, None, None)
    return jax.shard_map(on_device, mesh=mesh, in_specs=in_specs, out_specs=out_specs, check_vma=False)
```

```python
import jax
import jax.numpy as jnp
from jax import lax
from jax.experimental import pallas as pl
from jax.experimental.pallas import tpu as pltpu
from jax.sharding import PartitionSpec as P

MESH = pl.DeviceIdType.MESH
SIDE = 4
PEERS = 128
GROUPS = 3
PHASES = 2
PICKS = 2
REMOTE = PEERS * PICKS
CHUNK = 4


def coords(device):
    return [device // 32, (device // 8) % 4, (device // 2) % 4, device % 2]


def index_of(position):
    y, z, x, core = position
    return ((y * 4 + z) * 4 + x) * 2 + core


def shifted(position, axis, steps, core_flip=0):
    moved = list(position)
    moved[axis] = (moved[axis] + steps) % SIDE
    if core_flip:
        moved[3] = 1 - moved[3]
    return index_of(moved)


def axes_of(group):
    return group, (group + 1) % 3, (group + 2) % 3


def fused_kernel(picks, own_wants, fields, weights, out, landing, want_rows, *scratch):
    count = GROUPS * PHASES
    near = [scratch[i * SIDE : (i + 1) * SIDE] for i in range(count)]
    scratch = scratch[count * SIDE :]
    bundle, scratch = scratch[:GROUPS], scratch[GROUPS:]
    pool, scratch = scratch[:count], scratch[count:]
    wants, tiles, result, *sems = scratch
    meta_send, meta_recv, own_sem, a_send, a_recv, b_send, b_recv, c_first, c_send, c_recv, keep_sem, w_sem, o_sem = sems
    blocks, _, group_rows, _ = fields.shape
    half = blocks // 2
    rows = group_rows // PHASES
    here = coords(lax.axis_index("region"))

    def send(src, dst, send_sem, recv_sem, device):
        copy = pltpu.make_async_remote_copy(
            src_ref=src, dst_ref=dst, send_sem=send_sem, recv_sem=recv_sem, device_id=(device,), device_id_type=MESH
        )
        copy.start()
        return copy

    def await_bytes(ref, sem):
        pltpu.make_async_copy(ref, ref, sem).wait()

    def keep(src, dst, sem):
        copy = pltpu.make_async_copy(src, dst, sem)
        copy.start()
        return copy

    def fetch_tiles(chunk, slot):
        return keep(weights.at[pl.ds(chunk * CHUNK, CHUNK)], tiles.at[slot], w_sem.at[slot])

    fetch_tiles(0, 0)
    own_copies = [
        keep(fields.at[:, k % GROUPS, pl.ds(k // GROUPS * rows, rows), :], near[k][0], own_sem.at[k])
        for k in range(count)
    ]
    own_row = keep(own_wants, want_rows.at[0], meta_send.at[13])

    peers = [shifted(here, axis, steps, flip) for axis in range(3) for steps in (1, 2, 3) for flip in (0, 1)]
    peers.append(shifted(here, 0, 0, 1))
    barrier = pltpu.get_barrier_semaphore()
    for peer in peers:
        pl.semaphore_signal(barrier, inc=1, device_id=(peer,), device_id_type=MESH)
    pl.semaphore_wait(barrier, len(peers))

    def send_wants_z():
        copies = []
        for steps in range(SIDE):
            for flip in (0, 1):
                if steps or flip:
                    row = (SIDE - steps) % SIDE * 2 + flip
                    peer = shifted(here, 1, steps, flip)
                    copies.append(
                        send(own_wants, want_rows.at[row], meta_send.at[len(copies)], meta_recv.at[0], peer)
                    )
        return copies

    def send_wants(axis, first_sem, known, stage):
        return [
            send(
                want_rows.at[pl.ds(0, known)],
                want_rows.at[pl.ds((SIDE - steps) * known, known)],
                meta_send.at[first_sem + steps - 1],
                meta_recv.at[stage],
                shifted(here, axis, steps),
            )
            for steps in (1, 2, 3)
        ]

    low, high = pl.ds(0, half), pl.ds(half, half)

    def start_gather(k):
        phase, group = divmod(k, GROUPS)
        part = pl.ds(phase * rows, rows)
        up, down = shifted(here, group, 1), shifted(here, group, 3)
        plan = (
            (low, near[k][3], up),
            (high, near[k][1], down),
            (high, near[k][3], up),
            (low, near[k][1], down),
        )
        return [
            send(fields.at[span, group, part, :], dst.at[span], a_send.at[k, i], a_recv.at[k, i], device)
            for i, (span, dst, device) in enumerate(plan)
        ]

    def relay_gather(k, copies):
        group = k % GROUPS
        up, down = shifted(here, group, 1), shifted(here, group, 3)
        copies[0].wait_recv()
        copies.append(send(near[k][3].at[low], near[k][2].at[low], a_send.at[k, 4], a_recv.at[k, 4], up))
        copies[1].wait_recv()
        copies.append(send(near[k][1].at[high], near[k][2].at[high], a_send.at[k, 5], a_recv.at[k, 5], down))

    def pick(k, ja, tb):
        group = k % GROUPS
        axis_a, axis_b, axis_c = axes_of(group)
        source = list(here)
        source[axis_a] = (source[axis_a] + ja) % SIDE
        column = index_of(source)

        def one(t, carry):
            away = [0, 0, 0]
            away[axis_b] = tb
            away[axis_c] = t // 2
            row = ((away[0] * 4 + away[2]) * 4 + away[1]) * 2 + t % 2
            for r in range(PICKS):
                bundle[group][tb, t, ja * PICKS + r] = near[k][ja][wants[row, r, column]]
            return carry

        lax.fori_loop(0, 2 * SIDE, one, 0)

    def send_bundle(k, tb):
        jb = SIDE - tb
        _, axis_b, _ = axes_of(k % GROUPS)
        return send(
            bundle[k % GROUPS].at[tb],
            landing.at[k, jb - 1],
            b_send.at[k, tb - 1],
            b_recv.at[k, jb - 1],
            shifted(here, axis_b, tb),
        )

    def send_on(k, jb):
        group = k % GROUPS
        _, _, axis_c = axes_of(group)
        for t in (4, 5, 2, 3, 6, 7, 1, 0):
            tc, flip = divmod(t, 2)
            src = bundle[group].at[0, t] if jb == 0 else landing.at[k, jb - 1, t]
            jc = (SIDE - tc) % SIDE
            dst = pool[k].at[pl.ds(((jb * SIDE + jc) * 2 + flip) * 8, 8)]
            if t == 0:
                keep(src, dst, keep_sem.at[k, jb])
            else:
                sent = c_send.at[k, t - 1] if jb else c_first.at[k, t - 1]
                send(src, dst, sent, c_recv.at[k, jc], shifted(here, axis_c, tc, flip))

    def await_kept(k, jb):
        await_bytes(pool[k].at[pl.ds(0, 8)], keep_sem.at[k, jb])

    def free_bundle(k, along):
        for copy in along.values():
            copy.wait_send()
        for t in range(1, 2 * SIDE):
            await_bytes(pool[k].at[pl.ds(0, 8)], c_first.at[k, t - 1])
        await_kept(k, 0)

    def await_pool(k):
        for jc in range(SIDE):
            await_bytes(pool[k].at[pl.ds(0, 64 if jc else 32)], c_recv.at[k, jc])
        for jb in range(1, SIDE):
            await_kept(k, jb)

    def interpolate(phase):
        chunks = blocks // CHUNK
        part = pl.ds(phase * rows, rows)

        def write_back(chunk, slot):
            span = pl.ds(chunk * CHUNK, CHUNK)
            return pltpu.make_async_copy(result.at[slot], out.at[span, :, part, :], o_sem.at[slot])

        def source(b, s):
            parts = []
            for group in range(GROUPS):
                k = phase * GROUPS + group
                at = picks[group, b, s]
                away = pool[k][jnp.minimum(at, REMOTE - 1)]
                local = near[k][0][jnp.maximum(at - REMOTE, 0)]
                parts.append(jnp.where(at < REMOTE, away, local))
            return jnp.concatenate(parts, axis=0)

        def one(chunk, carry):
            slot = chunk % 2
            await_bytes(tiles.at[slot], w_sem.at[slot])

            @pl.when(chunk + 1 < chunks)
            def _():
                fetch_tiles(chunk + 1, 1 - slot)

            @pl.when(chunk >= 2)
            def _():
                write_back(chunk - 2, slot).wait()

            for i in range(CHUNK):
                b = chunk * CHUNK + i
                total = None
                for s in range(0, weights.shape[1], 2):
                    left = jnp.concatenate([source(b, s), source(b, s + 1)], axis=1)
                    right = tiles[slot, i, s : s + 2].reshape(2 * weights.shape[2], weights.shape[3])
                    dot = jnp.dot(left, right, preferred_element_type=jnp.float32)
                    total = dot if total is None else total + dot
                total = total.astype(out.dtype)
                for group in range(GROUPS):
                    result[slot, i, group] = total[group * rows : (group + 1) * rows]
            write_back(chunk, slot).start()
            return carry

        lax.fori_loop(0, chunks, one, 0)
        for chunk in (chunks - 2, chunks - 1):
            write_back(chunk, chunk % 2).wait()

    gathered, along = {}, {}
    meta = send_wants_z()
    for k in range(GROUPS):
        gathered[k] = start_gather(k)
    own_row.wait()
    await_bytes(want_rows.at[pl.ds(0, 7)], meta_recv.at[0])
    meta += send_wants(2, 7, 8, 1)
    for k in range(GROUPS):
        relay_gather(k, gathered[k])
    await_bytes(want_rows.at[pl.ds(0, 24)], meta_recv.at[1])
    meta += send_wants(0, 10, 32, 2)
    for copy in own_copies:
        copy.wait()
    await_bytes(want_rows.at[pl.ds(0, 96)], meta_recv.at[2])
    table = keep(want_rows, wants, meta_send.at[13])
    table.wait()

    for phase in range(PHASES):
        ks = range(phase * GROUPS, (phase + 1) * GROUPS)
        for k in ks:
            if phase:
                free_bundle(k - GROUPS, along[k - GROUPS])
            for tb in range(SIDE):
                pick(k, 0, tb)
        for k in ks:
            gathered[k][3].wait_recv()
            for tb in range(SIDE):
                pick(k, 1, tb)
            gathered[k][2].wait_recv()
            for tb in range(SIDE):
                pick(k, 3, tb)
        for k in ks:
            gathered[k][4].wait_recv()
            gathered[k][5].wait_recv()
            if phase + 1 < PHASES:
                gathered[k + GROUPS] = start_gather(k + GROUPS)
        for k in ks:
            along[k] = {}
            for tb in (2, 1, 3, 0):
                pick(k, 2, tb)
                if tb:
                    along[k][SIDE - tb] = send_bundle(k, tb)
            send_on(k, 0)
        if phase + 1 < PHASES:
            for k in ks:
                relay_gather(k + GROUPS, gathered[k + GROUPS])
        for jb in (1, 3, 2):
            for k in ks:
                along[k][jb].wait_recv()
                send_on(k, jb)

    for phase in range(PHASES):
        for k in range(phase * GROUPS, (phase + 1) * GROUPS):
            await_pool(k)
            if phase == PHASES - 1:
                free_bundle(k, along[k])
        if phase:
            fetch_tiles(0, 0)
        interpolate(phase)

    for copy in meta:
        copy.wait_send()
    for k in range(count):
        for copy in gathered[k]:
            copy.wait_send()
        for t in range(1, 2 * SIDE):
            await_bytes(pool[k].at[pl.ds(0, 24)], c_send.at[k, t - 1])


def fused(picks, wants, fields, weights):
    blocks, _, group_rows, cols = fields.shape
    rows = group_rows // PHASES
    count = GROUPS * PHASES
    kind = fields.dtype
    dma = pltpu.SemaphoreType.DMA
    any_spec = pl.BlockSpec(memory_space=pl.ANY)
    scratch = [pltpu.VMEM((blocks, rows, cols), kind) for _ in range(count * SIDE)]
    scratch += [pltpu.VMEM((SIDE, 2 * SIDE, SIDE * PICKS, rows, cols), kind) for _ in range(GROUPS)]
    scratch += [pltpu.VMEM((REMOTE, rows, cols), kind) for _ in range(count)]
    scratch += [
        pltpu.SMEM((PEERS, PICKS, PEERS), jnp.int32),
        pltpu.VMEM((2, CHUNK) + weights.shape[1:], kind),
        pltpu.VMEM((2, CHUNK, GROUPS, rows, cols), kind),
        dma((14,)),
        dma((3,)),
        dma((count,)),
        dma((count, 6)),
        dma((count, 6)),
        dma((count, 3)),
        dma((count, 3)),
        dma((count, 7)),
        dma((count, 7)),
        dma((count, SIDE)),
        dma((count, SIDE)),
        dma((2,)),
        dma((2,)),
    ]
    return pl.pallas_call(
        fused_kernel,
        out_shape=(
            jax.ShapeDtypeStruct(fields.shape, kind),
            jax.ShapeDtypeStruct((count, SIDE - 1, 2 * SIDE, SIDE * PICKS, rows, cols), kind),
            jax.ShapeDtypeStruct((PEERS, PICKS, PEERS), jnp.int32),
        ),
        in_specs=[pl.BlockSpec(memory_space=pltpu.SMEM), any_spec, any_spec, any_spec],
        out_specs=(any_spec, any_spec, any_spec),
        scratch_shapes=scratch,
        compiler_params=pltpu.CompilerParams(
            collective_id=0, has_side_effects=True, vmem_limit_bytes=62 * 1024 * 1024
        ),
    )(picks, wants, fields, weights)[0]


def tables(departures, blocks):
    me = lax.axis_index("region")
    flat = departures.reshape(-1)
    owner = flat // blocks
    local = flat % blocks
    key = jnp.arange(flat.shape[0], dtype=jnp.int32) * 64 + local
    named = owner[None, :] == jnp.arange(PEERS, dtype=jnp.int32)[:, None]
    first = jnp.min(jnp.where(named, key[None, :], 1 << 30), axis=1)
    last = jnp.max(jnp.where(named, key[None, :], 0), axis=1)
    wants = jnp.stack([jnp.where(first < (1 << 30), first, 0) % 64, last % 64], axis=0)
    is_first = jnp.any(named & (key[None, :] == first[:, None]), axis=0)
    rank = jnp.where(is_first, 0, 1)
    there, here = coords(owner), coords(me)
    away = [(there[i] - here[i]) % SIDE for i in range(3)]
    flip = (there[3] - here[3]) % 2
    picks = []
    for group in range(GROUPS):
        ja, jb, jc = (away[axis] for axis in axes_of(group))
        spot = (((jb * SIDE + jc) * 2 + flip) * SIDE + ja) * PICKS + rank
        picks.append(jnp.where(owner == me, REMOTE + local, spot))
    return wants, jnp.stack(picks).reshape((GROUPS,) + departures.shape)


def on_device(fields, weights, departures):
    blocks, field_count, levels, cols = fields.shape
    grouped = fields.reshape(blocks, GROUPS, field_count // GROUPS * levels, cols)
    wants, picks = tables(departures, blocks)
    return fused(picks, wants, grouped, weights).reshape(fields.shape)


def solution(mesh):
    in_specs = (P("region", None, None, None), P("region", None, None, None), P("region", None))
    out_specs = P("region", None, None, None)
    return jax.shard_map(on_device, mesh=mesh, in_specs=in_specs, out_specs=out_specs, check_vma=False)
```

```python
import jax
import jax.numpy as jnp
from jax import lax
from jax.experimental import pallas as pl
from jax.experimental.pallas import tpu as pltpu
from jax.sharding import PartitionSpec as P

MESH = pl.DeviceIdType.MESH
SIDE = 4
PEERS = 128
GROUPS = 3
PHASES = 4
BUNDLES = 2
PICKS = 2
REMOTE = PEERS * PICKS
CHUNK = 6
SLOTS = 4


def coords(device):
    return [device // 32, (device // 8) % 4, (device // 2) % 4, device % 2]


def index_of(position):
    y, z, x, core = position
    return ((y * 4 + z) * 4 + x) * 2 + core


def shifted(position, axis, steps, core_flip=0):
    moved = list(position)
    moved[axis] = (moved[axis] + steps) % SIDE
    if core_flip:
        moved[3] = 1 - moved[3]
    return index_of(moved)


def axes_of(group):
    return group, (group + 1) % 3, (group + 2) % 3


def fused_kernel(picks, own_wants, fields, weights, out, landing, want_rows, *scratch):
    count = GROUPS * PHASES
    near = [scratch[i * SIDE : (i + 1) * SIDE] for i in range(count)]
    scratch = scratch[count * SIDE :]
    bundle, scratch = scratch[: GROUPS * BUNDLES], scratch[GROUPS * BUNDLES :]
    pool, scratch = scratch[:count], scratch[count:]
    wants, tiles, result, *sems = scratch
    meta_send, meta_recv, own_sem, a_send, a_recv, b_send, b_recv, c_first, c_send, c_recv, keep_sem, w_sem, o_sem = sems
    blocks, _, group_rows, _ = fields.shape
    half = blocks // 2
    rows = group_rows // PHASES
    here = coords(lax.axis_index("region"))

    def bundle_of(k):
        return bundle[k % (GROUPS * BUNDLES)]

    def send(src, dst, send_sem, recv_sem, device):
        copy = pltpu.make_async_remote_copy(
            src_ref=src, dst_ref=dst, send_sem=send_sem, recv_sem=recv_sem, device_id=(device,), device_id_type=MESH
        )
        copy.start()
        return copy

    def await_bytes(ref, sem):
        pltpu.make_async_copy(ref, ref, sem).wait()

    def keep(src, dst, sem):
        copy = pltpu.make_async_copy(src, dst, sem)
        copy.start()
        return copy

    def fetch_tiles(chunk, slot):
        return keep(weights.at[pl.ds(chunk * CHUNK, CHUNK)], tiles.at[slot], w_sem.at[slot])

    for step in range(SLOTS - 1):
        fetch_tiles(step, step)
    own_copies = [
        keep(fields.at[:, k % GROUPS, pl.ds(k // GROUPS * rows, rows), :], near[k][0], own_sem.at[k])
        for k in range(count)
    ]
    own_row = keep(own_wants, want_rows.at[0], meta_send.at[13])

    peers = [shifted(here, axis, steps, flip) for axis in range(3) for steps in (1, 2, 3) for flip in (0, 1)]
    peers.append(shifted(here, 0, 0, 1))
    barrier = pltpu.get_barrier_semaphore()
    for peer in peers:
        pl.semaphore_signal(barrier, inc=1, device_id=(peer,), device_id_type=MESH)
    pl.semaphore_wait(barrier, len(peers))

    def send_wants_z():
        copies = []
        for steps in range(SIDE):
            for flip in (0, 1):
                if steps or flip:
                    row = (SIDE - steps) % SIDE * 2 + flip
                    peer = shifted(here, 1, steps, flip)
                    copies.append(
                        send(own_wants, want_rows.at[row], meta_send.at[len(copies)], meta_recv.at[0], peer)
                    )
        return copies

    def send_wants(axis, first_sem, known, stage):
        return [
            send(
                want_rows.at[pl.ds(0, known)],
                want_rows.at[pl.ds((SIDE - steps) * known, known)],
                meta_send.at[first_sem + steps - 1],
                meta_recv.at[stage],
                shifted(here, axis, steps),
            )
            for steps in (1, 2, 3)
        ]

    low, high = pl.ds(0, half), pl.ds(half, half)

    def start_gather(k):
        phase, group = divmod(k, GROUPS)
        part = pl.ds(phase * rows, rows)
        up, down = shifted(here, group, 1), shifted(here, group, 3)
        plan = (
            (low, near[k][3], up),
            (high, near[k][1], down),
            (high, near[k][3], up),
            (low, near[k][1], down),
        )
        return [
            send(fields.at[span, group, part, :], dst.at[span], a_send.at[k, i], a_recv.at[k, i], device)
            for i, (span, dst, device) in enumerate(plan)
        ]

    def relay_gather(k, copies):
        group = k % GROUPS
        up, down = shifted(here, group, 1), shifted(here, group, 3)
        copies[0].wait_recv()
        copies.append(send(near[k][3].at[low], near[k][2].at[low], a_send.at[k, 4], a_recv.at[k, 4], up))
        copies[1].wait_recv()
        copies.append(send(near[k][1].at[high], near[k][2].at[high], a_send.at[k, 5], a_recv.at[k, 5], down))

    def pick(k, ja, tbs):
        group = k % GROUPS
        axis_a, axis_b, axis_c = axes_of(group)
        source = list(here)
        source[axis_a] = (source[axis_a] + ja) % SIDE
        column = index_of(source)

        def one(t, carry):
            for tb in tbs:
                away = [0, 0, 0]
                away[axis_b] = tb
                away[axis_c] = t // 2
                row = ((away[0] * 4 + away[2]) * 4 + away[1]) * 2 + t % 2
                for r in range(PICKS):
                    bundle_of(k)[tb, t, ja * PICKS + r] = near[k][ja][wants[row, r, column]]
            return carry

        lax.fori_loop(0, 2 * SIDE, one, 0)

    def send_bundle(k, tb):
        jb = SIDE - tb
        _, axis_b, _ = axes_of(k % GROUPS)
        return send(
            bundle_of(k).at[tb],
            landing.at[k, jb - 1],
            b_send.at[k, tb - 1],
            b_recv.at[k, jb - 1],
            shifted(here, axis_b, tb),
        )

    def send_on(k, jb):
        _, _, axis_c = axes_of(k % GROUPS)
        for t in (4, 5, 2, 3, 6, 7, 1, 0):
            tc, flip = divmod(t, 2)
            src = bundle_of(k).at[0, t] if jb == 0 else landing.at[k, jb - 1, t]
            jc = (SIDE - tc) % SIDE
            dst = pool[k].at[pl.ds(((jb * SIDE + jc) * 2 + flip) * 8, 8)]
            if t == 0:
                keep(src, dst, keep_sem.at[k, jb])
            else:
                sent = c_send.at[k, t - 1] if jb else c_first.at[k, t - 1]
                send(src, dst, sent, c_recv.at[k, jc], shifted(here, axis_c, tc, flip))

    def await_kept(k, jb):
        await_bytes(pool[k].at[pl.ds(0, 8)], keep_sem.at[k, jb])

    def free_bundle(k, along):
        for copy in along.values():
            copy.wait_send()
        for t in range(1, 2 * SIDE):
            await_bytes(pool[k].at[pl.ds(0, 8)], c_first.at[k, t - 1])
        await_kept(k, 0)

    def await_pool(k):
        for jc in range(SIDE):
            await_bytes(pool[k].at[pl.ds(0, 64 if jc else 32)], c_recv.at[k, jc])
        for jb in range(1, SIDE):
            await_kept(k, jb)

    def interpolate(phase):
        chunks = blocks // CHUNK
        part = pl.ds(phase * rows, rows)

        def write_back(chunk, slot):
            span = pl.ds(chunk * CHUNK, CHUNK)
            return pltpu.make_async_copy(result.at[slot], out.at[span, :, part, :], o_sem.at[slot])

        def source(b, s):
            parts = []
            for group in range(GROUPS):
                k = phase * GROUPS + group
                at = picks[group, b, s]
                away = pool[k][jnp.minimum(at, REMOTE - 1)]
                local = near[k][0][jnp.maximum(at - REMOTE, 0)]
                parts.append(jnp.where(at < REMOTE, away, local))
            return jnp.concatenate(parts, axis=0)

        def one(chunk, carry):
            slot = chunk % 2
            now, later = chunk % SLOTS, chunk + SLOTS - 1
            await_bytes(tiles.at[now], w_sem.at[now])

            @pl.when(later < chunks)
            def _():
                fetch_tiles(later, later % SLOTS)

            @pl.when(chunk >= 2)
            def _():
                write_back(chunk - 2, slot).wait()

            for i in range(CHUNK):
                b = chunk * CHUNK + i
                total = None
                for s in range(0, weights.shape[1], 2):
                    left = jnp.concatenate([source(b, s), source(b, s + 1)], axis=1)
                    right = tiles[now, i, s : s + 2].reshape(2 * weights.shape[2], weights.shape[3])
                    dot = jnp.dot(left, right, preferred_element_type=jnp.float32)
                    total = dot if total is None else total + dot
                total = total.astype(out.dtype)
                for group in range(GROUPS):
                    result[slot, i, group] = total[group * rows : (group + 1) * rows]
            write_back(chunk, slot).start()
            return carry

        lax.fori_loop(0, chunks, one, 0)
        for chunk in (chunks - 2, chunks - 1):
            write_back(chunk, chunk % 2).wait()

    def groups_of(phase):
        return range(phase * GROUPS, (phase + 1) * GROUPS)

    def start_phase(phase):
        if phase < PHASES:
            for k in groups_of(phase):
                gathered[k] = start_gather(k)

    def relay_phase(phase):
        if phase < PHASES:
            for k in groups_of(phase):
                relay_gather(k, gathered[k])

    def pick_phase(phase):
        ks = groups_of(phase)
        every = range(SIDE)
        for k in ks:
            if phase >= BUNDLES:
                before = k - GROUPS * BUNDLES
                free_bundle(before, along[before])
            pick(k, 0, every)
        for k in ks:
            gathered[k][3].wait_recv()
            pick(k, 1, every)
            gathered[k][2].wait_recv()
            pick(k, 3, every)
        for k in ks:
            along[k] = {}
            gathered[k][4].wait_recv()
            gathered[k][5].wait_recv()
            for tb in (2, 1, 3, 0):
                pick(k, 2, (tb,))
                if tb:
                    along[k][SIDE - tb] = send_bundle(k, tb)
            send_on(k, 0)

    def forward_phase(phase):
        for jb in (1, 3, 2):
            for k in groups_of(phase):
                along[k][jb].wait_recv()
                send_on(k, jb)

    def finish_phase(phase):
        if phase:
            for step in range(SLOTS - 1):
                fetch_tiles(step, step)
        for k in groups_of(phase):
            await_pool(k)
            if phase >= PHASES - BUNDLES:
                free_bundle(k, along[k])
        interpolate(phase)

    gathered, along = {}, {}
    meta = send_wants_z()
    start_phase(0)
    own_row.wait()
    await_bytes(want_rows.at[pl.ds(0, 7)], meta_recv.at[0])
    meta += send_wants(2, 7, 8, 1)
    relay_phase(0)
    await_bytes(want_rows.at[pl.ds(0, 24)], meta_recv.at[1])
    meta += send_wants(0, 10, 32, 2)
    start_phase(1)
    for copy in own_copies:
        copy.wait()
    await_bytes(want_rows.at[pl.ds(0, 96)], meta_recv.at[2])
    keep(want_rows, wants, meta_send.at[13]).wait()

    for step in range(PHASES + 2):
        if step < PHASES:
            pick_phase(step)
            relay_phase(step + 1)
            start_phase(step + 2)
        if 1 <= step <= PHASES:
            forward_phase(step - 1)
        if step >= 2:
            finish_phase(step - 2)

    for copy in meta:
        copy.wait_send()
    for k in range(count):
        for copy in gathered[k]:
            copy.wait_send()
        for t in range(1, 2 * SIDE):
            await_bytes(pool[k].at[pl.ds(0, 24)], c_send.at[k, t - 1])


def fused(picks, wants, fields, weights):
    blocks, _, group_rows, cols = fields.shape
    rows = group_rows // PHASES
    count = GROUPS * PHASES
    kind = fields.dtype
    dma = pltpu.SemaphoreType.DMA
    any_spec = pl.BlockSpec(memory_space=pl.ANY)
    scratch = [pltpu.VMEM((blocks, rows, cols), kind) for _ in range(count * SIDE)]
    scratch += [pltpu.VMEM((SIDE, 2 * SIDE, SIDE * PICKS, rows, cols), kind) for _ in range(GROUPS * BUNDLES)]
    scratch += [pltpu.VMEM((REMOTE, rows, cols), kind) for _ in range(count)]
    scratch += [
        pltpu.SMEM((PEERS, PICKS, PEERS), jnp.int32),
        pltpu.VMEM((SLOTS, CHUNK) + weights.shape[1:], kind),
        pltpu.VMEM((2, CHUNK, GROUPS, rows, cols), kind),
        dma((14,)),
        dma((3,)),
        dma((count,)),
        dma((count, 6)),
        dma((count, 6)),
        dma((count, 3)),
        dma((count, 3)),
        dma((count, 7)),
        dma((count, 7)),
        dma((count, SIDE)),
        dma((count, SIDE)),
        dma((SLOTS,)),
        dma((2,)),
    ]
    return pl.pallas_call(
        fused_kernel,
        out_shape=(
            jax.ShapeDtypeStruct(fields.shape, kind),
            jax.ShapeDtypeStruct((count, SIDE - 1, 2 * SIDE, SIDE * PICKS, rows, cols), kind),
            jax.ShapeDtypeStruct((PEERS, PICKS, PEERS), jnp.int32),
        ),
        in_specs=[pl.BlockSpec(memory_space=pltpu.SMEM), any_spec, any_spec, any_spec],
        out_specs=(any_spec, any_spec, any_spec),
        scratch_shapes=scratch,
        compiler_params=pltpu.CompilerParams(
            collective_id=0, has_side_effects=True, vmem_limit_bytes=62 * 1024 * 1024
        ),
    )(picks, wants, fields, weights)[0]


def tables(departures, blocks):
    me = lax.axis_index("region")
    flat = departures.reshape(-1)
    owner = flat // blocks
    local = flat % blocks
    key = jnp.arange(flat.shape[0], dtype=jnp.int32) * 64 + local
    named = owner[None, :] == jnp.arange(PEERS, dtype=jnp.int32)[:, None]
    first = jnp.min(jnp.where(named, key[None, :], 1 << 30), axis=1)
    last = jnp.max(jnp.where(named, key[None, :], 0), axis=1)
    wants = jnp.stack([jnp.where(first < (1 << 30), first, 0) % 64, last % 64], axis=0)
    is_first = jnp.any(named & (key[None, :] == first[:, None]), axis=0)
    rank = jnp.where(is_first, 0, 1)
    there, here = coords(owner), coords(me)
    away = [(there[i] - here[i]) % SIDE for i in range(3)]
    flip = (there[3] - here[3]) % 2
    picks = []
    for group in range(GROUPS):
        ja, jb, jc = (away[axis] for axis in axes_of(group))
        spot = (((jb * SIDE + jc) * 2 + flip) * SIDE + ja) * PICKS + rank
        picks.append(jnp.where(owner == me, REMOTE + local, spot))
    return wants, jnp.stack(picks).reshape((GROUPS,) + departures.shape)


def on_device(fields, weights, departures):
    blocks, field_count, levels, cols = fields.shape
    grouped = fields.reshape(blocks, GROUPS, field_count // GROUPS * levels, cols)
    wants, picks = tables(departures, blocks)
    return fused(picks, wants, grouped, weights).reshape(fields.shape)


def solution(mesh):
    in_specs = (P("region", None, None, None), P("region", None, None, None), P("region", None))
    out_specs = P("region", None, None, None)
    return jax.shard_map(on_device, mesh=mesh, in_specs=in_specs, out_specs=out_specs, check_vma=False)
```

```python
import jax
import jax.numpy as jnp
from jax import lax
from jax.experimental import pallas as pl
from jax.experimental.pallas import tpu as pltpu
from jax.sharding import PartitionSpec as P

MESH = pl.DeviceIdType.MESH
SIDE = 4
PEERS = 128
GROUPS = 3
PHASES = 4
BUNDLES = 2
PICKS = 2
REMOTE = PEERS * PICKS
CHUNK = 6
STORES = 8
SLOTS = 4


def coords(device):
    return [device // 32, (device // 8) % 4, (device // 2) % 4, device % 2]


def index_of(position):
    y, z, x, core = position
    return ((y * 4 + z) * 4 + x) * 2 + core


def shifted(position, axis, steps, core_flip=0):
    moved = list(position)
    moved[axis] = (moved[axis] + steps) % SIDE
    if core_flip:
        moved[3] = 1 - moved[3]
    return index_of(moved)


def axes_of(group):
    return group, (group + 1) % 3, (group + 2) % 3


def fused_kernel(departures, fields, weights, out, landing, want_rows, *scratch):
    count = GROUPS * PHASES
    near = [scratch[i * SIDE : (i + 1) * SIDE] for i in range(count)]
    scratch = scratch[count * SIDE :]
    bundle, scratch = scratch[: GROUPS * BUNDLES], scratch[GROUPS * BUNDLES :]
    pool, scratch = scratch[:count], scratch[count:]
    wants, picks, own_wants, spots, tiles, result, *sems = scratch
    meta_send, meta_recv, own_sem, a_send, a_recv, b_send, b_recv, c_first, c_send, c_recv, keep_sem, w_sem, o_sem = sems
    blocks, _, group_rows, _ = fields.shape
    half = blocks // 2
    rows = group_rows // PHASES
    here = coords(lax.axis_index("region"))

    def bundle_of(k):
        return bundle[k % (GROUPS * BUNDLES)]

    def send(src, dst, send_sem, recv_sem, device):
        copy = pltpu.make_async_remote_copy(
            src_ref=src, dst_ref=dst, send_sem=send_sem, recv_sem=recv_sem, device_id=(device,), device_id_type=MESH
        )
        copy.start()
        return copy

    def await_bytes(ref, sem):
        pltpu.make_async_copy(ref, ref, sem).wait()

    def keep(src, dst, sem):
        copy = pltpu.make_async_copy(src, dst, sem)
        copy.start()
        return copy

    def fetch_tiles(chunk, slot):
        return keep(weights.at[pl.ds(chunk * CHUNK, CHUNK)], tiles.at[slot], w_sem.at[slot])

    for step in range(SLOTS - 1):
        fetch_tiles(step, step)
    own_copies = [
        keep(fields.at[:, k % GROUPS, pl.ds(k // GROUPS * rows, rows), :], near[k][0], own_sem.at[k])
        for k in range(count)
    ]

    peers = [shifted(here, axis, steps, flip) for axis in range(3) for steps in (1, 2, 3) for flip in (0, 1)]
    peers.append(shifted(here, 0, 0, 1))
    barrier = pltpu.get_barrier_semaphore()
    for peer in peers:
        pl.semaphore_signal(barrier, inc=1, device_id=(peer,), device_id_type=MESH)

    def tables():
        ids = departures[...]
        slots = ids.shape[1]
        lane = lax.broadcasted_iota(jnp.int32, (blocks, PEERS), 1)
        block = lax.broadcasted_iota(jnp.int32, (blocks, PEERS), 0)

        def spread(columns):
            wide = jnp.zeros((blocks, PEERS), jnp.int32)
            for s, column in enumerate(columns):
                wide = jnp.where(lane % slots == s, column, wide)
            return wide

        owner = (ids * 43691) >> 21
        local = ids - owner * blocks
        keys, named = [], []
        first = jnp.full((blocks, PEERS), 1 << 30, jnp.int32)
        last = jnp.zeros((blocks, PEERS), jnp.int32)
        for s in range(slots):
            key = (block * slots + s) * 64 + local[:, s : s + 1]
            keys.append(key)
            named.append(owner[:, s : s + 1] == lane)
            first = jnp.minimum(first, jnp.where(named[s], key, 1 << 30))
            last = jnp.maximum(last, jnp.where(named[s], key, 0))
        first = jnp.min(first, axis=0, keepdims=True)
        last = jnp.max(last, axis=0, keepdims=True)
        own_wants[0:1] = first % 64
        own_wants[1:2] = last % 64
        ranks = []
        for s in range(slots):
            later = jnp.where(named[s], jnp.where(keys[s] == first, 0, 1), 0)
            ranks.append(jnp.max(later, axis=1, keepdims=True))
        rank = spread(ranks)
        owner = spread([owner[:, s : s + 1] for s in range(slots)])
        local = spread([local[:, s : s + 1] for s in range(slots)])
        there = (owner >> 5, (owner >> 3) & 3, (owner >> 1) & 3)
        away = [(there[i] - here[i]) & 3 for i in range(3)]
        flip = (owner - here[3]) & 1
        group = lane // slots

        def along_axis(which):
            a, b, c = (axes_of(g)[which] for g in range(GROUPS))
            return jnp.where(group == 0, away[a], jnp.where(group == 1, away[b], away[c]))

        spot = (((along_axis(1) * SIDE + along_axis(2)) * 2 + flip) * SIDE + along_axis(0)) * PICKS + rank
        spots[...] = jnp.where(owner == lax.axis_index("region"), REMOTE + local, spot)

    tables()
    own_row = keep(own_wants, want_rows.at[0], meta_send.at[13])
    pick_table = keep(spots, picks, meta_send.at[14])
    pl.semaphore_wait(barrier, len(peers))

    def send_wants_z():
        copies = []
        for steps in range(SIDE):
            for flip in (0, 1):
                if steps or flip:
                    row = (SIDE - steps) % SIDE * 2 + flip
                    peer = shifted(here, 1, steps, flip)
                    copies.append(
                        send(own_wants, want_rows.at[row], meta_send.at[len(copies)], meta_recv.at[0], peer)
                    )
        return copies

    def send_wants(axis, first_sem, known, stage):
        return [
            send(
                want_rows.at[pl.ds(0, known)],
                want_rows.at[pl.ds((SIDE - steps) * known, known)],
                meta_send.at[first_sem + steps - 1],
                meta_recv.at[stage],
                shifted(here, axis, steps),
            )
            for steps in (1, 2, 3)
        ]

    low, high = pl.ds(0, half), pl.ds(half, half)

    def start_gather(k):
        phase, group = divmod(k, GROUPS)
        part = pl.ds(phase * rows, rows)
        up, down = shifted(here, group, 1), shifted(here, group, 3)
        plan = (
            (low, near[k][3], up),
            (high, near[k][1], down),
            (high, near[k][3], up),
            (low, near[k][1], down),
        )
        return [
            send(fields.at[span, group, part, :], dst.at[span], a_send.at[k, i], a_recv.at[k, i], device)
            for i, (span, dst, device) in enumerate(plan)
        ]

    def relay_gather(k, copies):
        group = k % GROUPS
        up, down = shifted(here, group, 1), shifted(here, group, 3)
        copies[0].wait_recv()
        copies.append(send(near[k][3].at[low], near[k][2].at[low], a_send.at[k, 4], a_recv.at[k, 4], up))
        copies[1].wait_recv()
        copies.append(send(near[k][1].at[high], near[k][2].at[high], a_send.at[k, 5], a_recv.at[k, 5], down))

    def pick(k, ja, tbs):
        group = k % GROUPS
        axis_a, axis_b, axis_c = axes_of(group)
        source = list(here)
        source[axis_a] = (source[axis_a] + ja) % SIDE
        column = index_of(source)

        def one(t, carry):
            for tb in tbs:
                away = [0, 0, 0]
                away[axis_b] = tb
                away[axis_c] = t // 2
                row = ((away[0] * 4 + away[2]) * 4 + away[1]) * 2 + t % 2
                for r in range(PICKS):
                    bundle_of(k)[tb, t, ja * PICKS + r] = near[k][ja][wants[row, r, column]]
            return carry

        lax.fori_loop(0, 2 * SIDE, one, 0)

    def send_bundle(k, tb):
        jb = SIDE - tb
        _, axis_b, _ = axes_of(k % GROUPS)
        return send(
            bundle_of(k).at[tb],
            landing.at[k, jb - 1],
            b_send.at[k, tb - 1],
            b_recv.at[k, jb - 1],
            shifted(here, axis_b, tb),
        )

    def send_on(k, jb):
        _, _, axis_c = axes_of(k % GROUPS)
        for t in (4, 5, 2, 3, 6, 7, 1, 0):
            tc, flip = divmod(t, 2)
            src = bundle_of(k).at[0, t] if jb == 0 else landing.at[k, jb - 1, t]
            jc = (SIDE - tc) % SIDE
            dst = pool[k].at[pl.ds(((jb * SIDE + jc) * 2 + flip) * 8, 8)]
            if t == 0:
                keep(src, dst, keep_sem.at[k, jb])
            else:
                sent = c_send.at[k, t - 1] if jb else c_first.at[k, t - 1]
                send(src, dst, sent, c_recv.at[k, jc], shifted(here, axis_c, tc, flip))

    def await_kept(k, jb):
        await_bytes(pool[k].at[pl.ds(0, 8)], keep_sem.at[k, jb])

    def free_bundle(k, along):
        for copy in along.values():
            copy.wait_send()
        for t in range(1, 2 * SIDE):
            await_bytes(pool[k].at[pl.ds(0, 8)], c_first.at[k, t - 1])
        await_kept(k, 0)

    def await_pool(k):
        for jc in range(SIDE):
            await_bytes(pool[k].at[pl.ds(0, 64 if jc else 32)], c_recv.at[k, jc])
        for jb in range(1, SIDE):
            await_kept(k, jb)

    def interpolate(phase):
        chunks = blocks // CHUNK
        part = pl.ds(phase * rows, rows)

        def write_back(chunk, slot):
            span = pl.ds(chunk * CHUNK, CHUNK)
            return pltpu.make_async_copy(result.at[slot], out.at[span, :, part, :], o_sem.at[slot])

        def source(b, s):
            parts = []
            for group in range(GROUPS):
                k = phase * GROUPS + group
                at = picks[b, group * weights.shape[1] + s]
                away = pool[k][jnp.minimum(at, REMOTE - 1)]
                local = near[k][0][jnp.maximum(at - REMOTE, 0)]
                parts.append(jnp.where(at < REMOTE, away, local))
            return jnp.concatenate(parts, axis=0)

        def one(chunk, carry):
            slot = chunk % 2
            now, later = chunk % SLOTS, chunk + SLOTS - 1
            await_bytes(tiles.at[now], w_sem.at[now])

            @pl.when(later < chunks)
            def _():
                fetch_tiles(later, later % SLOTS)

            @pl.when(chunk >= 2)
            def _():
                write_back(chunk - 2, slot).wait()

            for i in range(CHUNK):
                b = chunk * CHUNK + i
                total = None
                for s in range(0, weights.shape[1], 2):
                    left = jnp.concatenate([source(b, s), source(b, s + 1)], axis=1)
                    right = tiles[now, i, s : s + 2].reshape(2 * weights.shape[2], weights.shape[3])
                    dot = jnp.dot(left, right, preferred_element_type=jnp.float32)
                    total = dot if total is None else total + dot
                total = total.astype(out.dtype)
                for group in range(GROUPS):
                    result[slot, i, group] = total[group * rows : (group + 1) * rows]
            write_back(chunk, slot).start()
            return carry

        lax.fori_loop(0, chunks, one, 0)
        for chunk in (chunks - 2, chunks - 1):
            write_back(chunk, chunk % 2).wait()

    def groups_of(phase):
        return range(phase * GROUPS, (phase + 1) * GROUPS)

    def start_phase(phase):
        if phase < PHASES:
            for k in groups_of(phase):
                gathered[k] = start_gather(k)

    def relay_phase(phase):
        if phase < PHASES:
            for k in groups_of(phase):
                relay_gather(k, gathered[k])

    def pick_phase(phase):
        ks = groups_of(phase)
        every = range(SIDE)
        for k in ks:
            if phase >= BUNDLES:
                before = k - GROUPS * BUNDLES
                free_bundle(before, along[before])
            pick(k, 0, every)
        for k in ks:
            gathered[k][3].wait_recv()
            pick(k, 1, every)
            gathered[k][2].wait_recv()
            pick(k, 3, every)
        for k in ks:
            along[k] = {}
            gathered[k][4].wait_recv()
            gathered[k][5].wait_recv()
            for tb in (2, 1, 3, 0):
                pick(k, 2, (tb,))
                if tb:
                    along[k][SIDE - tb] = send_bundle(k, tb)
            send_on(k, 0)

    def forward_phase(phase):
        for jb in (1, 3, 2):
            for k in groups_of(phase):
                along[k][jb].wait_recv()
                send_on(k, jb)

    def finish_phase(phase):
        if phase:
            for step in range(SLOTS - 1):
                fetch_tiles(step, step)
        for k in groups_of(phase):
            await_pool(k)
            if phase >= PHASES - BUNDLES:
                free_bundle(k, along[k])
        interpolate(phase)

    gathered, along = {}, {}
    meta = send_wants_z()
    start_phase(0)
    own_row.wait()
    pick_table.wait()
    await_bytes(want_rows.at[pl.ds(0, 7)], meta_recv.at[0])
    meta += send_wants(2, 7, 8, 1)
    relay_phase(0)
    await_bytes(want_rows.at[pl.ds(0, 24)], meta_recv.at[1])
    meta += send_wants(0, 10, 32, 2)
    start_phase(1)
    for copy in own_copies:
        copy.wait()
    await_bytes(want_rows.at[pl.ds(0, 96)], meta_recv.at[2])
    keep(want_rows, wants, meta_send.at[13]).wait()

    for step in range(PHASES + 2):
        if step < PHASES:
            pick_phase(step)
            relay_phase(step + 1)
            start_phase(step + 2)
        if 1 <= step <= PHASES:
            forward_phase(step - 1)
        if step >= 2:
            finish_phase(step - 2)

    for copy in meta:
        copy.wait_send()
    for k in range(count):
        for copy in gathered[k]:
            copy.wait_send()
        for t in range(1, 2 * SIDE):
            await_bytes(pool[k].at[pl.ds(0, 24)], c_send.at[k, t - 1])


def fused(departures, fields, weights):
    blocks, _, group_rows, cols = fields.shape
    rows = group_rows // PHASES
    count = GROUPS * PHASES
    kind = fields.dtype
    dma = pltpu.SemaphoreType.DMA
    any_spec = pl.BlockSpec(memory_space=pl.ANY)
    scratch = [pltpu.VMEM((blocks, rows, cols), kind) for _ in range(count * SIDE)]
    scratch += [pltpu.VMEM((SIDE, 2 * SIDE, SIDE * PICKS, rows, cols), kind) for _ in range(GROUPS * BUNDLES)]
    scratch += [pltpu.VMEM((REMOTE, rows, cols), kind) for _ in range(count)]
    scratch += [
        pltpu.SMEM((PEERS, PICKS, PEERS), jnp.int32),
        pltpu.SMEM((blocks, PEERS), jnp.int32),
        pltpu.VMEM((PICKS, PEERS), jnp.int32),
        pltpu.VMEM((blocks, PEERS), jnp.int32),
        pltpu.VMEM((SLOTS, CHUNK) + weights.shape[1:], kind),
        pltpu.VMEM((2, CHUNK, GROUPS, rows, cols), kind),
        dma((15,)),
        dma((3,)),
        dma((count,)),
        dma((count, 6)),
        dma((count, 6)),
        dma((count, 3)),
        dma((count, 3)),
        dma((count, 7)),
        dma((count, 7)),
        dma((count, SIDE)),
        dma((count, SIDE)),
        dma((SLOTS,)),
        dma((2,)),
    ]
    return pl.pallas_call(
        fused_kernel,
        out_shape=(
            jax.ShapeDtypeStruct(fields.shape, kind),
            jax.ShapeDtypeStruct((count, SIDE - 1, 2 * SIDE, SIDE * PICKS, rows, cols), kind),
            jax.ShapeDtypeStruct((PEERS, PICKS, PEERS), jnp.int32),
        ),
        in_specs=[pl.BlockSpec(memory_space=pltpu.VMEM), any_spec, any_spec],
        out_specs=(any_spec, any_spec, any_spec),
        scratch_shapes=scratch,
        compiler_params=pltpu.CompilerParams(
            collective_id=0, has_side_effects=True, vmem_limit_bytes=62 * 1024 * 1024
        ),
    )(departures, fields, weights)[0]


def store_kernel(src, dst, held, in_sems, out_sems):
    step = src.shape[0] // STORES
    spans = [pl.ds(i * step, step) for i in range(STORES)]
    loads = [pltpu.make_async_copy(src.at[span], held.at[span], in_sems.at[i]) for i, span in enumerate(spans)]
    stores = [pltpu.make_async_copy(held.at[span], dst.at[span], out_sems.at[i]) for i, span in enumerate(spans)]
    for copy in loads:
        copy.start()
    for i in range(STORES):
        loads[i].wait()
        stores[i].start()
    for copy in stores:
        copy.wait()


def store(result):
    any_spec = pl.BlockSpec(memory_space=pl.ANY)
    return pl.pallas_call(
        store_kernel,
        out_shape=jax.ShapeDtypeStruct(result.shape, result.dtype),
        in_specs=[any_spec],
        out_specs=any_spec,
        scratch_shapes=[
            pltpu.VMEM(result.shape, result.dtype),
            pltpu.SemaphoreType.DMA((STORES,)),
            pltpu.SemaphoreType.DMA((STORES,)),
        ],
        compiler_params=pltpu.CompilerParams(vmem_limit_bytes=60 * 1024 * 1024),
    )(result)


def on_device(fields, weights, departures):
    blocks, field_count, levels, cols = fields.shape
    grouped = fields.reshape(blocks, GROUPS, field_count // GROUPS * levels, cols)
    return store(fused(departures, grouped, weights)).reshape(fields.shape)


def solution(mesh):
    in_specs = (P("region", None, None, None), P("region", None, None, None), P("region", None))
    out_specs = P("region", None, None, None)
    return jax.shard_map(on_device, mesh=mesh, in_specs=in_specs, out_specs=out_specs, check_vma=False)
```

```python
import jax
import jax.numpy as jnp
from jax import lax
from jax.experimental import pallas as pl
from jax.experimental.pallas import tpu as pltpu
from jax.sharding import PartitionSpec as P

MESH = pl.DeviceIdType.MESH
SIDE = 4
PEERS = 128
GROUPS = 3
PHASES = 4
BUNDLES = 2
PICKS = 2
REMOTE = PEERS * PICKS
CHUNK = 6
STORES = 4
SLOTS = 4


def coords(device):
    return [device // 32, (device // 8) % 4, (device // 2) % 4, device % 2]


def index_of(position):
    y, z, x, core = position
    return ((y * 4 + z) * 4 + x) * 2 + core


def shifted(position, axis, steps, core_flip=0):
    moved = list(position)
    moved[axis] = (moved[axis] + steps) % SIDE
    if core_flip:
        moved[3] = 1 - moved[3]
    return index_of(moved)


def axes_of(group):
    return group, (group + 1) % 3, (group + 2) % 3


def fused_kernel(departures_home, fields, weights, out, landing, want_rows, *scratch):
    count = GROUPS * PHASES
    near = [scratch[i * SIDE : (i + 1) * SIDE] for i in range(count)]
    scratch = scratch[count * SIDE :]
    bundle, scratch = scratch[: GROUPS * BUNDLES], scratch[GROUPS * BUNDLES :]
    pool, scratch = scratch[:count], scratch[count:]
    wants, picks, own_wants, spots, departures, tiles, result, *sems = scratch
    meta_send, meta_recv, own_sem, a_send, a_recv, b_send, b_recv, c_first, c_send, c_recv, keep_sem, w_sem, o_sem = sems
    blocks, _, group_rows, _ = fields.shape
    half = blocks // 2
    rows = group_rows // PHASES
    here = coords(lax.axis_index("region"))

    def bundle_of(k):
        return bundle[k % (GROUPS * BUNDLES)]

    def send(src, dst, send_sem, recv_sem, device):
        copy = pltpu.make_async_remote_copy(
            src_ref=src, dst_ref=dst, send_sem=send_sem, recv_sem=recv_sem, device_id=(device,), device_id_type=MESH
        )
        copy.start()
        return copy

    def await_bytes(ref, sem):
        pltpu.make_async_copy(ref, ref, sem).wait()

    def keep(src, dst, sem):
        copy = pltpu.make_async_copy(src, dst, sem)
        copy.start()
        return copy

    def fetch_tiles(chunk, slot):
        return keep(weights.at[pl.ds(chunk * CHUNK, CHUNK)], tiles.at[slot], w_sem.at[slot])

    ids_copy = keep(departures_home, departures, meta_send.at[14])
    for step in range(SLOTS - 1):
        fetch_tiles(step, step)
    own_copies = [
        keep(fields.at[:, k % GROUPS, pl.ds(k // GROUPS * rows, rows), :], near[k][0], own_sem.at[k])
        for k in range(count)
    ]

    peers = [shifted(here, axis, steps, flip) for axis in range(3) for steps in (1, 2, 3) for flip in (0, 1)]
    peers.append(shifted(here, 0, 0, 1))
    barrier = pltpu.get_barrier_semaphore()
    for peer in peers:
        pl.semaphore_signal(barrier, inc=1, device_id=(peer,), device_id_type=MESH)

    def tables():
        ids = departures[...]
        slots = ids.shape[1]
        lane = lax.broadcasted_iota(jnp.int32, (blocks, PEERS), 1)
        block = lax.broadcasted_iota(jnp.int32, (blocks, PEERS), 0)

        def spread(columns):
            wide = jnp.zeros((blocks, PEERS), jnp.int32)
            for s, column in enumerate(columns):
                wide = jnp.where(lane % slots == s, column, wide)
            return wide

        owner = (ids * 43691) >> 21
        local = ids - owner * blocks
        keys, named = [], []
        first = jnp.full((blocks, PEERS), 1 << 30, jnp.int32)
        last = jnp.zeros((blocks, PEERS), jnp.int32)
        for s in range(slots):
            key = (block * slots + s) * 64 + local[:, s : s + 1]
            keys.append(key)
            named.append(owner[:, s : s + 1] == lane)
            first = jnp.minimum(first, jnp.where(named[s], key, 1 << 30))
            last = jnp.maximum(last, jnp.where(named[s], key, 0))
        first = jnp.min(first, axis=0, keepdims=True)
        last = jnp.max(last, axis=0, keepdims=True)
        own_wants[0:1] = first % 64
        own_wants[1:2] = last % 64
        ranks = []
        for s in range(slots):
            later = jnp.where(named[s], jnp.where(keys[s] == first, 0, 1), 0)
            ranks.append(jnp.max(later, axis=1, keepdims=True))
        rank = spread(ranks)
        owner = spread([owner[:, s : s + 1] for s in range(slots)])
        local = spread([local[:, s : s + 1] for s in range(slots)])
        there = (owner >> 5, (owner >> 3) & 3, (owner >> 1) & 3)
        away = [(there[i] - here[i]) & 3 for i in range(3)]
        flip = (owner - here[3]) & 1
        group = lane // slots

        def along_axis(which):
            a, b, c = (axes_of(g)[which] for g in range(GROUPS))
            return jnp.where(group == 0, away[a], jnp.where(group == 1, away[b], away[c]))

        spot = (((along_axis(1) * SIDE + along_axis(2)) * 2 + flip) * SIDE + along_axis(0)) * PICKS + rank
        spots[...] = jnp.where(owner == lax.axis_index("region"), REMOTE + local, spot)

    ids_copy.wait()
    tables()
    own_row = keep(own_wants, want_rows.at[0], meta_send.at[13])
    pick_table = keep(spots, picks, meta_send.at[14])
    pl.semaphore_wait(barrier, len(peers))

    def send_wants_z():
        copies = []
        for steps in range(SIDE):
            for flip in (0, 1):
                if steps or flip:
                    row = (SIDE - steps) % SIDE * 2 + flip
                    peer = shifted(here, 1, steps, flip)
                    copies.append(
                        send(own_wants, want_rows.at[row], meta_send.at[len(copies)], meta_recv.at[0], peer)
                    )
        return copies

    def send_wants(axis, first_sem, known, stage):
        return [
            send(
                want_rows.at[pl.ds(0, known)],
                want_rows.at[pl.ds((SIDE - steps) * known, known)],
                meta_send.at[first_sem + steps - 1],
                meta_recv.at[stage],
                shifted(here, axis, steps),
            )
            for steps in (1, 2, 3)
        ]

    low, high = pl.ds(0, half), pl.ds(half, half)

    def start_gather(k):
        phase, group = divmod(k, GROUPS)
        part = pl.ds(phase * rows, rows)
        up, down = shifted(here, group, 1), shifted(here, group, 3)
        plan = (
            (low, near[k][3], up),
            (high, near[k][1], down),
            (high, near[k][3], up),
            (low, near[k][1], down),
        )
        return [
            send(fields.at[span, group, part, :], dst.at[span], a_send.at[k, i], a_recv.at[k, i], device)
            for i, (span, dst, device) in enumerate(plan)
        ]

    def relay_gather(k, copies):
        group = k % GROUPS
        up, down = shifted(here, group, 1), shifted(here, group, 3)
        copies[0].wait_recv()
        copies.append(send(near[k][3].at[low], near[k][2].at[low], a_send.at[k, 4], a_recv.at[k, 4], up))
        copies[1].wait_recv()
        copies.append(send(near[k][1].at[high], near[k][2].at[high], a_send.at[k, 5], a_recv.at[k, 5], down))

    def pick(k, ja, tbs):
        group = k % GROUPS
        axis_a, axis_b, axis_c = axes_of(group)
        source = list(here)
        source[axis_a] = (source[axis_a] + ja) % SIDE
        column = index_of(source)

        def one(t, carry):
            for tb in tbs:
                away = [0, 0, 0]
                away[axis_b] = tb
                away[axis_c] = t // 2
                row = ((away[0] * 4 + away[2]) * 4 + away[1]) * 2 + t % 2
                for r in range(PICKS):
                    bundle_of(k)[tb, t, ja * PICKS + r] = near[k][ja][wants[row, r, column]]
            return carry

        lax.fori_loop(0, 2 * SIDE, one, 0)

    def send_bundle(k, tb):
        jb = SIDE - tb
        _, axis_b, _ = axes_of(k % GROUPS)
        return send(
            bundle_of(k).at[tb],
            landing.at[k, jb - 1],
            b_send.at[k, tb - 1],
            b_recv.at[k, jb - 1],
            shifted(here, axis_b, tb),
        )

    def send_on(k, jb):
        _, _, axis_c = axes_of(k % GROUPS)
        for t in (4, 5, 2, 3, 6, 7, 1, 0):
            tc, flip = divmod(t, 2)
            src = bundle_of(k).at[0, t] if jb == 0 else landing.at[k, jb - 1, t]
            jc = (SIDE - tc) % SIDE
            dst = pool[k].at[pl.ds(((jb * SIDE + jc) * 2 + flip) * 8, 8)]
            if t == 0:
                keep(src, dst, keep_sem.at[k, jb])
            else:
                sent = c_send.at[k, t - 1] if jb else c_first.at[k, t - 1]
                send(src, dst, sent, c_recv.at[k, jc], shifted(here, axis_c, tc, flip))

    def await_kept(k, jb):
        await_bytes(pool[k].at[pl.ds(0, 8)], keep_sem.at[k, jb])

    def free_bundle(k, along):
        for copy in along.values():
            copy.wait_send()
        for t in range(1, 2 * SIDE):
            await_bytes(pool[k].at[pl.ds(0, 8)], c_first.at[k, t - 1])
        await_kept(k, 0)

    def await_pool(k):
        for jc in range(SIDE):
            await_bytes(pool[k].at[pl.ds(0, 64 if jc else 32)], c_recv.at[k, jc])
        for jb in range(1, SIDE):
            await_kept(k, jb)

    def interpolate(phase):
        chunks = blocks // CHUNK
        part = pl.ds(phase * rows, rows)

        def write_back(chunk, slot):
            span = pl.ds(chunk * CHUNK, CHUNK)
            return pltpu.make_async_copy(result.at[slot], out.at[span, :, part, :], o_sem.at[slot])

        def source(b, s):
            parts = []
            for group in range(GROUPS):
                k = phase * GROUPS + group
                at = picks[b, group * weights.shape[1] + s]
                away = pool[k][jnp.minimum(at, REMOTE - 1)]
                local = near[k][0][jnp.maximum(at - REMOTE, 0)]
                parts.append(jnp.where(at < REMOTE, away, local))
            return jnp.concatenate(parts, axis=0)

        def one(chunk, carry):
            slot = chunk % 2
            now, later = chunk % SLOTS, chunk + SLOTS - 1
            await_bytes(tiles.at[now], w_sem.at[now])

            @pl.when(later < chunks)
            def _():
                fetch_tiles(later, later % SLOTS)

            @pl.when(chunk >= 2)
            def _():
                write_back(chunk - 2, slot).wait()

            for i in range(CHUNK):
                b = chunk * CHUNK + i
                total = None
                for s in range(0, weights.shape[1], 2):
                    left = jnp.concatenate([source(b, s), source(b, s + 1)], axis=1)
                    right = tiles[now, i, s : s + 2].reshape(2 * weights.shape[2], weights.shape[3])
                    dot = jnp.dot(left, right, preferred_element_type=jnp.float32)
                    total = dot if total is None else total + dot
                total = total.astype(out.dtype)
                for group in range(GROUPS):
                    result[slot, i, group] = total[group * rows : (group + 1) * rows]
            write_back(chunk, slot).start()
            return carry

        lax.fori_loop(0, chunks, one, 0)
        for chunk in (chunks - 2, chunks - 1):
            write_back(chunk, chunk % 2).wait()

    def groups_of(phase):
        return range(phase * GROUPS, (phase + 1) * GROUPS)

    def start_phase(phase):
        if phase < PHASES:
            for k in groups_of(phase):
                gathered[k] = start_gather(k)

    def relay_phase(phase):
        if phase < PHASES:
            for k in groups_of(phase):
                relay_gather(k, gathered[k])

    def pick_phase(phase):
        ks = groups_of(phase)
        every = range(SIDE)
        for k in ks:
            if phase >= BUNDLES:
                before = k - GROUPS * BUNDLES
                free_bundle(before, along[before])
            pick(k, 0, every)
        for k in ks:
            gathered[k][3].wait_recv()
            pick(k, 1, every)
            gathered[k][2].wait_recv()
            pick(k, 3, every)
        for k in ks:
            along[k] = {}
            gathered[k][4].wait_recv()
            gathered[k][5].wait_recv()
            for tb in (2, 1, 3, 0):
                pick(k, 2, (tb,))
                if tb:
                    along[k][SIDE - tb] = send_bundle(k, tb)
            send_on(k, 0)

    def forward_phase(phase):
        for jb in (1, 3, 2):
            for k in groups_of(phase):
                along[k][jb].wait_recv()
                send_on(k, jb)

    def finish_phase(phase):
        if phase:
            for step in range(SLOTS - 1):
                fetch_tiles(step, step)
        for k in groups_of(phase):
            await_pool(k)
            if phase >= PHASES - BUNDLES:
                free_bundle(k, along[k])
        interpolate(phase)

    gathered, along = {}, {}
    meta = send_wants_z()
    start_phase(0)
    own_row.wait()
    pick_table.wait()
    await_bytes(want_rows.at[pl.ds(0, 7)], meta_recv.at[0])
    meta += send_wants(2, 7, 8, 1)
    relay_phase(0)
    await_bytes(want_rows.at[pl.ds(0, 24)], meta_recv.at[1])
    meta += send_wants(0, 10, 32, 2)
    start_phase(1)
    for copy in own_copies:
        copy.wait()
    await_bytes(want_rows.at[pl.ds(0, 96)], meta_recv.at[2])
    keep(want_rows, wants, meta_send.at[13]).wait()

    for step in range(PHASES + 2):
        if step < PHASES:
            pick_phase(step)
            relay_phase(step + 1)
            start_phase(step + 2)
        if 1 <= step <= PHASES:
            forward_phase(step - 1)
        if step >= 2:
            finish_phase(step - 2)

    for copy in meta:
        copy.wait_send()
    for k in range(count):
        for copy in gathered[k]:
            copy.wait_send()
        for t in range(1, 2 * SIDE):
            await_bytes(pool[k].at[pl.ds(0, 24)], c_send.at[k, t - 1])


def fused(departures, fields, weights):
    blocks, _, group_rows, cols = fields.shape
    rows = group_rows // PHASES
    count = GROUPS * PHASES
    kind = fields.dtype
    dma = pltpu.SemaphoreType.DMA
    any_spec = pl.BlockSpec(memory_space=pl.ANY)
    scratch = [pltpu.VMEM((blocks, rows, cols), kind) for _ in range(count * SIDE)]
    scratch += [pltpu.VMEM((SIDE, 2 * SIDE, SIDE * PICKS, rows, cols), kind) for _ in range(GROUPS * BUNDLES)]
    scratch += [pltpu.VMEM((REMOTE, rows, cols), kind) for _ in range(count)]
    scratch += [
        pltpu.SMEM((PEERS, PICKS, PEERS), jnp.int32),
        pltpu.SMEM((blocks, PEERS), jnp.int32),
        pltpu.VMEM((PICKS, PEERS), jnp.int32),
        pltpu.VMEM((blocks, PEERS), jnp.int32),
        pltpu.VMEM(departures.shape, jnp.int32),
        pltpu.VMEM((SLOTS, CHUNK) + weights.shape[1:], kind),
        pltpu.VMEM((2, CHUNK, GROUPS, rows, cols), kind),
        dma((15,)),
        dma((3,)),
        dma((count,)),
        dma((count, 6)),
        dma((count, 6)),
        dma((count, 3)),
        dma((count, 3)),
        dma((count, 7)),
        dma((count, 7)),
        dma((count, SIDE)),
        dma((count, SIDE)),
        dma((SLOTS,)),
        dma((2,)),
    ]
    return pl.pallas_call(
        fused_kernel,
        out_shape=(
            jax.ShapeDtypeStruct(fields.shape, kind),
            jax.ShapeDtypeStruct((count, SIDE - 1, 2 * SIDE, SIDE * PICKS, rows, cols), kind),
            jax.ShapeDtypeStruct((PEERS, PICKS, PEERS), jnp.int32),
        ),
        in_specs=[any_spec, any_spec, any_spec],
        out_specs=(any_spec, any_spec, any_spec),
        scratch_shapes=scratch,
        compiler_params=pltpu.CompilerParams(
            collective_id=0, has_side_effects=True, vmem_limit_bytes=62 * 1024 * 1024
        ),
    )(departures, fields, weights)[0]


def store_kernel(src, dst, held, in_sems, out_sems):
    step = src.shape[0] // STORES
    spans = [pl.ds(i * step, step) for i in range(STORES)]
    loads = [pltpu.make_async_copy(src.at[span], held.at[span], in_sems.at[i]) for i, span in enumerate(spans)]
    stores = [pltpu.make_async_copy(held.at[span], dst.at[span], out_sems.at[i]) for i, span in enumerate(spans)]
    for copy in loads:
        copy.start()
    for i in range(STORES):
        loads[i].wait()
        stores[i].start()
    for copy in stores:
        copy.wait()


def store(result):
    any_spec = pl.BlockSpec(memory_space=pl.ANY)
    return pl.pallas_call(
        store_kernel,
        out_shape=jax.ShapeDtypeStruct(result.shape, result.dtype),
        in_specs=[any_spec],
        out_specs=any_spec,
        scratch_shapes=[
            pltpu.VMEM(result.shape, result.dtype),
            pltpu.SemaphoreType.DMA((STORES,)),
            pltpu.SemaphoreType.DMA((STORES,)),
        ],
        compiler_params=pltpu.CompilerParams(vmem_limit_bytes=60 * 1024 * 1024),
    )(result)


def on_device(fields, weights, departures):
    blocks, field_count, levels, cols = fields.shape
    grouped = fields.reshape(blocks, GROUPS, field_count // GROUPS * levels, cols)
    return store(fused(departures, grouped, weights)).reshape(fields.shape)


def solution(mesh):
    in_specs = (P("region", None, None, None), P("region", None, None, None), P("region", None))
    out_specs = P("region", None, None, None)
    return jax.shard_map(on_device, mesh=mesh, in_specs=in_specs, out_specs=out_specs, check_vma=False)
```

```python
import jax
import jax.numpy as jnp
from jax import lax
from jax.experimental import pallas as pl
from jax.experimental.pallas import tpu as pltpu
from jax.sharding import PartitionSpec as P

MESH = pl.DeviceIdType.MESH
SIDE = 4
PEERS = 128
GROUPS = 3
PHASES = 4
BUNDLES = 2
PICKS = 2
REMOTE = PEERS * PICKS
CHUNK = 6
STORES = 4
SLOTS = 4


def coords(device):
    return [device // 32, (device // 8) % 4, (device // 2) % 4, device % 2]


def index_of(position):
    y, z, x, core = position
    return ((y * 4 + z) * 4 + x) * 2 + core


def shifted(position, axis, steps, core_flip=0):
    moved = list(position)
    moved[axis] = (moved[axis] + steps) % SIDE
    if core_flip:
        moved[3] = 1 - moved[3]
    return index_of(moved)


def axes_of(group):
    return group, (group + 1) % 3, (group + 2) % 3


def fused_kernel(departures_home, fields, weights, out, landing, want_rows, *scratch):
    count = GROUPS * PHASES
    near = [scratch[i * SIDE : (i + 1) * SIDE] for i in range(count)]
    scratch = scratch[count * SIDE :]
    bundle, scratch = scratch[: GROUPS * BUNDLES], scratch[GROUPS * BUNDLES :]
    pool, scratch = scratch[:count], scratch[count:]
    wants, picks, own_wants, spots, departures, tiles, result, *sems = scratch
    meta_send, meta_recv, own_sem, a_send, a_recv, b_send, b_recv, c_first, c_send, c_recv, keep_sem, w_sem, o_sem = sems
    blocks, _, group_rows, _ = fields.shape
    half = blocks // 2
    rows = group_rows // PHASES
    here = coords(lax.axis_index("region"))

    def bundle_of(k):
        return bundle[k % (GROUPS * BUNDLES)]

    def send(src, dst, send_sem, recv_sem, device):
        copy = pltpu.make_async_remote_copy(
            src_ref=src, dst_ref=dst, send_sem=send_sem, recv_sem=recv_sem, device_id=(device,), device_id_type=MESH
        )
        copy.start()
        return copy

    def await_bytes(ref, sem):
        pltpu.make_async_copy(ref, ref, sem).wait()

    def keep(src, dst, sem):
        copy = pltpu.make_async_copy(src, dst, sem)
        copy.start()
        return copy

    def fetch_tiles(chunk, slot):
        return keep(weights.at[pl.ds(chunk * CHUNK, CHUNK)], tiles.at[slot], w_sem.at[slot])

    ids_copy = keep(departures_home, departures, meta_send.at[14])
    for step in range(SLOTS - 1):
        fetch_tiles(step, step)
    own_copies = [
        keep(fields.at[:, k % GROUPS, pl.ds(k // GROUPS * rows, rows), :], near[k][0], own_sem.at[k])
        for k in range(count)
    ]

    peers = [shifted(here, axis, steps, flip) for axis in range(3) for steps in (1, 2, 3) for flip in (0, 1)]
    peers.append(shifted(here, 0, 0, 1))
    barrier = pltpu.get_barrier_semaphore()
    for peer in peers:
        pl.semaphore_signal(barrier, inc=1, device_id=(peer,), device_id_type=MESH)

    def tables():
        ids = departures[...]
        slots = ids.shape[1]
        lane = lax.broadcasted_iota(jnp.int32, (blocks, PEERS), 1)
        block = lax.broadcasted_iota(jnp.int32, (blocks, PEERS), 0)

        def spread(columns):
            wide = jnp.zeros((blocks, PEERS), jnp.int32)
            for s, column in enumerate(columns):
                wide = jnp.where(lane % slots == s, column, wide)
            return wide

        owner = (ids * 43691) >> 21
        local = ids - owner * blocks
        keys, named = [], []
        first = jnp.full((blocks, PEERS), 1 << 30, jnp.int32)
        last = jnp.zeros((blocks, PEERS), jnp.int32)
        for s in range(slots):
            key = (block * slots + s) * 64 + local[:, s : s + 1]
            keys.append(key)
            named.append(owner[:, s : s + 1] == lane)
            first = jnp.minimum(first, jnp.where(named[s], key, 1 << 30))
            last = jnp.maximum(last, jnp.where(named[s], key, 0))
        first = jnp.min(first, axis=0, keepdims=True)
        last = jnp.max(last, axis=0, keepdims=True)
        own_wants[0:1] = first % 64
        own_wants[1:2] = last % 64
        ranks = []
        for s in range(slots):
            later = jnp.where(named[s], jnp.where(keys[s] == first, 0, 1), 0)
            ranks.append(jnp.max(later, axis=1, keepdims=True))
        rank = spread(ranks)
        owner = spread([owner[:, s : s + 1] for s in range(slots)])
        local = spread([local[:, s : s + 1] for s in range(slots)])
        there = (owner >> 5, (owner >> 3) & 3, (owner >> 1) & 3)
        away = [(there[i] - here[i]) & 3 for i in range(3)]
        flip = (owner - here[3]) & 1
        group = lane // slots

        def along_axis(which):
            a, b, c = (axes_of(g)[which] for g in range(GROUPS))
            return jnp.where(group == 0, away[a], jnp.where(group == 1, away[b], away[c]))

        spot = (((along_axis(1) * SIDE + along_axis(2)) * 2 + flip) * SIDE + along_axis(0)) * PICKS + rank
        spots[...] = jnp.where(owner == lax.axis_index("region"), REMOTE + local, spot)

    ids_copy.wait()
    tables()
    own_row = keep(own_wants, want_rows.at[0], meta_send.at[13])
    pick_table = keep(spots, picks, meta_send.at[14])
    pl.semaphore_wait(barrier, len(peers))

    def send_wants_z():
        copies = []
        for steps in range(SIDE):
            for flip in (0, 1):
                if steps or flip:
                    row = (SIDE - steps) % SIDE * 2 + flip
                    peer = shifted(here, 1, steps, flip)
                    copies.append(
                        send(own_wants, want_rows.at[row], meta_send.at[len(copies)], meta_recv.at[0], peer)
                    )
        return copies

    def send_wants(axis, first_sem, known, stage):
        return [
            send(
                want_rows.at[pl.ds(0, known)],
                want_rows.at[pl.ds((SIDE - steps) * known, known)],
                meta_send.at[first_sem + steps - 1],
                meta_recv.at[stage],
                shifted(here, axis, steps),
            )
            for steps in (1, 2, 3)
        ]

    low, high = pl.ds(0, half), pl.ds(half, half)

    def start_gather(k):
        phase, group = divmod(k, GROUPS)
        part = pl.ds(phase * rows, rows)
        up, down = shifted(here, group, 1), shifted(here, group, 3)
        plan = (
            (low, near[k][3], up),
            (high, near[k][1], down),
            (high, near[k][3], up),
            (low, near[k][1], down),
        )
        return [
            send(fields.at[span, group, part, :], dst.at[span], a_send.at[k, i], a_recv.at[k, i], device)
            for i, (span, dst, device) in enumerate(plan)
        ]

    def relay_gather(k, copies):
        group = k % GROUPS
        up, down = shifted(here, group, 1), shifted(here, group, 3)
        copies[0].wait_recv()
        copies.append(send(near[k][3].at[low], near[k][2].at[low], a_send.at[k, 4], a_recv.at[k, 4], up))
        copies[1].wait_recv()
        copies.append(send(near[k][1].at[high], near[k][2].at[high], a_send.at[k, 5], a_recv.at[k, 5], down))

    def pick(k, ja, tbs):
        group = k % GROUPS
        axis_a, axis_b, axis_c = axes_of(group)
        source = list(here)
        source[axis_a] = (source[axis_a] + ja) % SIDE
        column = index_of(source)

        def one(t, carry):
            for tb in tbs:
                away = [0, 0, 0]
                away[axis_b] = tb
                away[axis_c] = t // 2
                row = ((away[0] * 4 + away[2]) * 4 + away[1]) * 2 + t % 2
                for r in range(PICKS):
                    bundle_of(k)[tb, t, ja * PICKS + r] = near[k][ja][wants[row, r, column]]
            return carry

        lax.fori_loop(0, 2 * SIDE, one, 0)

    def send_bundle(k, tb):
        jb = SIDE - tb
        _, axis_b, _ = axes_of(k % GROUPS)
        return send(
            bundle_of(k).at[tb],
            landing.at[k, jb - 1],
            b_send.at[k, tb - 1],
            b_recv.at[k, jb - 1],
            shifted(here, axis_b, tb),
        )

    def send_on(k, jb):
        _, _, axis_c = axes_of(k % GROUPS)
        for t in (4, 5, 2, 3, 6, 7, 1, 0):
            tc, flip = divmod(t, 2)
            src = bundle_of(k).at[0, t] if jb == 0 else landing.at[k, jb - 1, t]
            jc = (SIDE - tc) % SIDE
            dst = pool[k].at[pl.ds(((jb * SIDE + jc) * 2 + flip) * 8, 8)]
            if t == 0:
                keep(src, dst, keep_sem.at[k, jb])
            else:
                sent = c_send.at[k, t - 1] if jb else c_first.at[k, t - 1]
                send(src, dst, sent, c_recv.at[k, jc], shifted(here, axis_c, tc, flip))

    def await_kept(k, jb):
        await_bytes(pool[k].at[pl.ds(0, 8)], keep_sem.at[k, jb])

    def free_bundle(k, along):
        for copy in along.values():
            copy.wait_send()
        for t in range(1, 2 * SIDE):
            await_bytes(pool[k].at[pl.ds(0, 8)], c_first.at[k, t - 1])
        await_kept(k, 0)

    def await_pool(k):
        for jc in range(SIDE):
            await_bytes(pool[k].at[pl.ds(0, 64 if jc else 32)], c_recv.at[k, jc])
        for jb in range(1, SIDE):
            await_kept(k, jb)

    def interpolate(phase):
        chunks = blocks // CHUNK
        part = pl.ds(phase * rows, rows)

        def write_back(chunk, slot):
            span = pl.ds(chunk * CHUNK, CHUNK)
            return pltpu.make_async_copy(result.at[slot], out.at[span, :, part, :], o_sem.at[slot])

        def source(b, s):
            parts = []
            for group in range(GROUPS):
                k = phase * GROUPS + group
                at = picks[b, group * weights.shape[1] + s]
                away = pool[k][jnp.minimum(at, REMOTE - 1)]
                local = near[k][0][jnp.maximum(at - REMOTE, 0)]
                parts.append(jnp.where(at < REMOTE, away, local))
            return jnp.concatenate(parts, axis=0)

        def one(chunk, carry):
            slot = chunk % 2
            now, later = chunk % SLOTS, chunk + SLOTS - 1
            await_bytes(tiles.at[now], w_sem.at[now])

            @pl.when(later < chunks)
            def _():
                fetch_tiles(later, later % SLOTS)

            @pl.when(chunk >= 2)
            def _():
                write_back(chunk - 2, slot).wait()

            for i in range(CHUNK):
                b = chunk * CHUNK + i
                total = None
                for s in range(0, weights.shape[1], 2):
                    left = jnp.concatenate([source(b, s), source(b, s + 1)], axis=1)
                    right = tiles[now, i, s : s + 2].reshape(2 * weights.shape[2], weights.shape[3])
                    dot = jnp.dot(left, right, preferred_element_type=jnp.float32)
                    total = dot if total is None else total + dot
                total = total.astype(out.dtype)
                for group in range(GROUPS):
                    result[slot, i, group] = total[group * rows : (group + 1) * rows]
            write_back(chunk, slot).start()
            return carry

        lax.fori_loop(0, chunks, one, 0)
        for chunk in (chunks - 2, chunks - 1):
            write_back(chunk, chunk % 2).wait()

    def groups_of(phase):
        return range(phase * GROUPS, (phase + 1) * GROUPS)

    def start_phase(phase):
        if phase < PHASES:
            for k in groups_of(phase):
                gathered[k] = start_gather(k)

    def relay_phase(phase):
        if phase < PHASES:
            for k in groups_of(phase):
                relay_gather(k, gathered[k])

    def pick_phase(phase):
        ks = groups_of(phase)
        every = range(SIDE)
        for k in ks:
            if phase >= BUNDLES:
                before = k - GROUPS * BUNDLES
                free_bundle(before, along[before])
            pick(k, 0, every)
        for k in ks:
            gathered[k][3].wait_recv()
            pick(k, 1, every)
            gathered[k][2].wait_recv()
            pick(k, 3, every)
        for k in ks:
            along[k] = {}
            gathered[k][4].wait_recv()
            gathered[k][5].wait_recv()
            for tb in (2, 1, 3, 0):
                pick(k, 2, (tb,))
                if tb:
                    along[k][SIDE - tb] = send_bundle(k, tb)
            send_on(k, 0)

    def forward_phase(phase):
        for jb in (1, 3, 2):
            for k in groups_of(phase):
                along[k][jb].wait_recv()
                send_on(k, jb)

    def finish_phase(phase):
        if phase:
            for step in range(SLOTS - 1):
                fetch_tiles(step, step)
        for k in groups_of(phase):
            await_pool(k)
            if phase >= PHASES - BUNDLES:
                free_bundle(k, along[k])
        interpolate(phase)

    gathered, along = {}, {}
    meta = send_wants_z()
    start_phase(0)
    own_row.wait()
    pick_table.wait()
    await_bytes(want_rows.at[pl.ds(0, 7)], meta_recv.at[0])
    meta += send_wants(2, 7, 8, 1)
    relay_phase(0)
    await_bytes(want_rows.at[pl.ds(0, 24)], meta_recv.at[1])
    meta += send_wants(0, 10, 32, 2)
    start_phase(1)
    for copy in own_copies:
        copy.wait()
    await_bytes(want_rows.at[pl.ds(0, 96)], meta_recv.at[2])
    keep(want_rows, wants, meta_send.at[13]).wait()

    for step in range(PHASES + 2):
        if step < PHASES:
            relay_phase(step + 1)
            start_phase(step + 2)
            pick_phase(step)
        if 1 <= step <= PHASES:
            forward_phase(step - 1)
        if step >= 2:
            finish_phase(step - 2)

    for copy in meta:
        copy.wait_send()
    for k in range(count):
        for copy in gathered[k]:
            copy.wait_send()
        for t in range(1, 2 * SIDE):
            await_bytes(pool[k].at[pl.ds(0, 24)], c_send.at[k, t - 1])


def fused(departures, fields, weights):
    blocks, _, group_rows, cols = fields.shape
    rows = group_rows // PHASES
    count = GROUPS * PHASES
    kind = fields.dtype
    dma = pltpu.SemaphoreType.DMA
    any_spec = pl.BlockSpec(memory_space=pl.ANY)
    scratch = [pltpu.VMEM((blocks, rows, cols), kind) for _ in range(count * SIDE)]
    scratch += [pltpu.VMEM((SIDE, 2 * SIDE, SIDE * PICKS, rows, cols), kind) for _ in range(GROUPS * BUNDLES)]
    scratch += [pltpu.VMEM((REMOTE, rows, cols), kind) for _ in range(count)]
    scratch += [
        pltpu.SMEM((PEERS, PICKS, PEERS), jnp.int32),
        pltpu.SMEM((blocks, PEERS), jnp.int32),
        pltpu.VMEM((PICKS, PEERS), jnp.int32),
        pltpu.VMEM((blocks, PEERS), jnp.int32),
        pltpu.VMEM(departures.shape, jnp.int32),
        pltpu.VMEM((SLOTS, CHUNK) + weights.shape[1:], kind),
        pltpu.VMEM((2, CHUNK, GROUPS, rows, cols), kind),
        dma((15,)),
        dma((3,)),
        dma((count,)),
        dma((count, 6)),
        dma((count, 6)),
        dma((count, 3)),
        dma((count, 3)),
        dma((count, 7)),
        dma((count, 7)),
        dma((count, SIDE)),
        dma((count, SIDE)),
        dma((SLOTS,)),
        dma((2,)),
    ]
    return pl.pallas_call(
        fused_kernel,
        out_shape=(
            jax.ShapeDtypeStruct(fields.shape, kind),
            jax.ShapeDtypeStruct((count, SIDE - 1, 2 * SIDE, SIDE * PICKS, rows, cols), kind),
            jax.ShapeDtypeStruct((PEERS, PICKS, PEERS), jnp.int32),
        ),
        in_specs=[any_spec, any_spec, any_spec],
        out_specs=(any_spec, any_spec, any_spec),
        scratch_shapes=scratch,
        compiler_params=pltpu.CompilerParams(
            collective_id=0, has_side_effects=True, vmem_limit_bytes=62 * 1024 * 1024
        ),
    )(departures, fields, weights)[0]


def store_kernel(src, dst, held, in_sems, out_sems):
    step = src.shape[0] // STORES
    spans = [pl.ds(i * step, step) for i in range(STORES)]
    loads = [pltpu.make_async_copy(src.at[span], held.at[span], in_sems.at[i]) for i, span in enumerate(spans)]
    stores = [pltpu.make_async_copy(held.at[span], dst.at[span], out_sems.at[i]) for i, span in enumerate(spans)]
    for copy in loads:
        copy.start()
    for i in range(STORES):
        loads[i].wait()
        stores[i].start()
    for copy in stores:
        copy.wait()


def store(result):
    any_spec = pl.BlockSpec(memory_space=pl.ANY)
    return pl.pallas_call(
        store_kernel,
        out_shape=jax.ShapeDtypeStruct(result.shape, result.dtype),
        in_specs=[any_spec],
        out_specs=any_spec,
        scratch_shapes=[
            pltpu.VMEM(result.shape, result.dtype),
            pltpu.SemaphoreType.DMA((STORES,)),
            pltpu.SemaphoreType.DMA((STORES,)),
        ],
        compiler_params=pltpu.CompilerParams(vmem_limit_bytes=60 * 1024 * 1024),
    )(result)


def on_device(fields, weights, departures):
    blocks, field_count, levels, cols = fields.shape
    grouped = fields.reshape(blocks, GROUPS, field_count // GROUPS * levels, cols)
    return store(fused(departures, grouped, weights)).reshape(fields.shape)


def solution(mesh):
    in_specs = (P("region", None, None, None), P("region", None, None, None), P("region", None))
    out_specs = P("region", None, None, None)
    return jax.shard_map(on_device, mesh=mesh, in_specs=in_specs, out_specs=out_specs, check_vma=False)
```
